32 devices in a mesh: seq: 8 (over y, x, core), exp: 4 (over z).
Axes of the slice: x: 2, y: 2, z: 4, core: 2. Of those that a mesh axis runs over, the one named last changes fastest.
Arguments:
- query_proj: bfloat16 [512, 4096], P('seq', 'exp'), may hold values from -6 to 6
- key_proj: bfloat16 [512, 4096], P('seq', 'exp'), may hold values from -6 to 6
- value_proj: bfloat16 [512, 4096], P('seq', 'exp'), may hold values from -6 to 6
- residual: bfloat16 [512, 6144], P(('seq', 'exp')), may hold values from -6 to 6
- out_weight: bfloat16 [6144, 4096], P('seq', 'exp'), may hold values from -0.09375 to 0.09375
- expert_ids: int32 [512, 2], P(('seq', 'exp')), may hold values from 0 to 3, all different within a row; in each aligned block of 16 rows (0 to 15, 16 to 31, ...) at most 12 rows name the same one
- gate_values: float32 [512, 2], P(('seq', 'exp')), may hold values from 0.2 to 1
- w_gate: bfloat16 [4, 9216, 6144], P('exp', 'seq'), may hold values from -0.078125 to 0.078125
- w_up: bfloat16 [4, 9216, 6144], P('exp', 'seq'), may hold values from -0.078125 to 0.078125
- w_down: bfloat16 [4, 9216, 6144], P('exp', 'seq'), may hold values from -0.0625 to 0.0625
Outputs:
- mixed: bfloat16 [512, 6144], P(('seq', 'exp'))
The draws below stay inside these ranges and needn't reach their ends.
Inputs may be any that keep to these rules, and one draw needn't show every extreme that they name: `expert_ids`: within the 16 rows of one device no expert is named more than 12 times, a bound that some block reaches; the 2 experts of a row differ.
All inputs are finite; a program needn't handle non-finite values.
Results may differ from the reference program's by a relative error of at most 0.018.
Values may be sent and summed in bfloat16 or wider, within the bound.
A program may use at most 128 MiB of HBM per device.

```python
import math
import jax
import jax.numpy as jnp
import numpy as np
from jax import lax

D = 6144
HEADS = 32
HD = 128
FF = 9216
TOP = 2
TOK_DEV = 64
TOKENS = 512
TOK_SUB = 16
EXPERTS = 4
HID_DEV = 1152
CAPS = 12
N_SEQ = 8
N_EXP = 4


def levels(rng, extent, split, low, largest):
    gain, own = 1.0, jax.random.fold_in(rng, 6)
    for axis_at, parts in split:
        heights = jnp.exp(jax.random.uniform(jax.random.fold_in(own, axis_at), (parts,), jnp.float32, low / len(split), largest / len(split)))
        gain = gain * jnp.repeat(heights, extent[axis_at] // parts).reshape([-1 if axis == axis_at else 1 for axis in range(len(extent))])
    return gain


def routed_block(rng, own, number, rows, amount, top, most, lean):
    order = jax.random.permutation(rng, amount)
    crowded, ordinary = portions_of(amount, rows * top, most, lean, True), portions_of(amount, rows * top, most, lean, False)
    places = jnp.arange(amount)

    def named(sizes, offset_by):
        used = int((sizes > 0).sum())
        fixed = max(1, used // 4)
        moved = fixed + (places - fixed + offset_by * (used - fixed)) % max(1, amount - fixed)
        return jnp.zeros((amount,), jnp.int32).at[order[jnp.where(places < fixed, places, moved)]].set(jnp.asarray(sizes, jnp.int32))

    sizes = jnp.where(number % 4 == 0, named(crowded, number // 4), named(ordinary, number - number // 4 - 1))
    mixed = jax.random.permutation(jax.random.fold_in(own, 3), amount)
    giver, sink = mixed[0:amount // 2 * 2:2], mixed[1:amount // 2 * 2:2]
    margin = jnp.minimum(sizes[giver] - 1, most - sizes[sink]) // 2
    margin = jnp.where((giver == order[0]) | (sink == order[0]) | (sizes[sink] == 0), 0, jnp.maximum(margin, 0))
    moved = jax.random.randint(jax.random.fold_in(own, 4), (amount // 2,), 0, 1 << 20) % (margin + 1)
    sizes = sizes.at[giver].add(-moved).at[sink].add(moved)
    members = jnp.searchsorted(jnp.cumsum(sizes), jnp.arange(rows * top), side="right").astype(jnp.int32)
    grid = members.reshape(top, rows).T
    grid = grid[jax.random.permutation(jax.random.fold_in(own, 1), rows)]
    offset_by = jax.random.randint(jax.random.fold_in(own, 2), (rows, 1), 0, top)
    return jnp.take_along_axis(grid, (jnp.arange(top)[None, :] + offset_by) % top, axis=1)


def portions_of(amount, total, reach, lean, full):
    loads = [(1 << 20) // math.isqrt(rank ** lean) + 1 for rank in range(1, amount + 1)]
    largest = reach if full else min(reach, max(-(-total // amount), total * loads[0] // sum(loads)))
    least = 1 if total - largest >= amount - 1 else 0
    holding, surplus = [largest] + [least] * (amount - 1), total - largest - least * (amount - 1)
    while surplus > 0:
        free = [i for i in range(1, amount) if holding[i] < largest] or [i for i in range(1, amount) if holding[i] < reach]
        whole, budget = sum([loads[i] for i in free]), surplus
        for i in free:
            addition = min(reach - holding[i], max(1, budget * loads[i] // whole), surplus)
            holding[i] = holding[i] + addition
            surplus = surplus - addition
    return np.array(holding)


def normal_values(key, extent, deviation, most, pieces=(), held_as=jnp.bfloat16):
    result = deviation * jax.random.normal(key, extent, jnp.float32)
    if pieces:
        result = result * levels(key, extent, pieces, -0.22, 0.18)
    return jnp.clip(result, -most, most).astype(held_as)


def setup_inputs(seed: int = 0) -> dict:
    key_of = jax.random.split(jax.random.key(seed), 11)
    query_proj = normal_values(key_of[0], (TOKENS, HEADS * HD), 1.0, 6.0, ((0, 8), (1, 4)))
    key_proj = normal_values(key_of[1], (TOKENS, HEADS * HD), 1.0, 6.0, ((0, 8), (1, 4)))
    value_proj = normal_values(key_of[2], (TOKENS, HEADS * HD), 1.0, 6.0, ((0, 8), (1, 4)))
    residual = normal_values(key_of[3], (TOKENS, D), 1.0, 6.0, ((0, 32),))
    out_weight = normal_values(key_of[4], (D, HEADS * HD), (HEADS * HD) ** -0.5, 0.09375, ((0, 8), (1, 4)))
    expert_ids_keys = jax.random.split(jax.random.fold_in(key_of[5], 1), TOKENS // TOK_SUB)
    expert_ids_turns = jax.random.permutation(jax.random.fold_in(key_of[5], 3), TOKENS // TOK_SUB)
    expert_ids = jax.vmap(lambda own, number: routed_block(jax.random.fold_in(key_of[5], 2), own, number, TOK_SUB, EXPERTS, TOP, CAPS, 2))(expert_ids_keys, expert_ids_turns).reshape((TOKENS, TOP))
    gate_values = jnp.clip(0.2 + 0.8 * jax.random.uniform(key_of[6], (TOKENS, TOP), jnp.float32) ** levels(key_of[6], (TOKENS, TOP), ((0, 32),), -0.2, 0.2), 0.2, 1.0)
    w_gate = normal_values(key_of[7], (EXPERTS, FF, D), D ** -0.5, 0.078125, ((0, 4), (1, 8)))
    w_up = normal_values(key_of[8], (EXPERTS, FF, D), D ** -0.5, 0.078125, ((0, 4), (1, 8)))
    w_down = normal_values(key_of[9], (EXPERTS, FF, D), FF ** -0.5, 0.0625, ((0, 4), (1, 8)))
    return {"query_proj": query_proj, "key_proj": key_proj, "value_proj": value_proj, "residual": residual, "out_weight": out_weight, "expert_ids": expert_ids, "gate_values": gate_values, "w_gate": w_gate, "w_up": w_up, "w_down": w_down}


def rounded(x):
    return lax.optimization_barrier(x.astype(jnp.bfloat16))

def features(x):
    widened = x.astype(jnp.float32)
    return rounded(widened * jax.nn.sigmoid(widened))

def times_rows(left, right):
    return lax.dot_general(left, right, (((1,), (1,)), ((), ())), preferred_element_type=jnp.float32)

def reference(query_proj, key_proj, value_proj, residual, out_weight, expert_ids, gate_values, w_gate, w_up, w_down):
    query_feat = features(query_proj).reshape(N_SEQ, TOK_DEV, HEADS, HD).astype(jnp.float32)
    key_feat = features(key_proj).reshape(N_SEQ, TOK_DEV, HEADS, HD).astype(jnp.float32)
    value_rows = value_proj.reshape(N_SEQ, TOK_DEV, HEADS, HD).astype(jnp.float32)
    states = jnp.einsum('cthd,cthe->chde', key_feat, value_rows)
    earlier = jnp.concatenate([jnp.zeros((1, HEADS, HD, HD), jnp.float32), jnp.cumsum(states, axis=0)[:-1]], axis=0)
    prefix = rounded(earlier).astype(jnp.float32)
    earlier_term = jnp.einsum('cthd,chde->cthe', query_feat, prefix)
    scores = jnp.einsum('cthd,cshd->chts', query_feat, key_feat)
    causal = jnp.arange(TOK_DEV)[:, None] >= jnp.arange(TOK_DEV)[None, :]
    weights = rounded(jnp.where(causal, scores, 0.0)).astype(jnp.float32)
    local_term = jnp.einsum('chts,cshe->cthe', weights, value_rows)
    combined = local_term + earlier_term
    normed = combined * lax.rsqrt(lax.optimization_barrier(jnp.mean(combined * combined, axis=-1, keepdims=True)) + 1e-06)
    normed = normed.astype(jnp.bfloat16).reshape(TOKENS, HEADS * HD)
    projected = times_rows(normed, out_weight)
    hidden_in = (residual.astype(jnp.float32) + projected).astype(jnp.bfloat16)
    blocks = N_SEQ * N_EXP
    chosen = expert_ids.reshape(blocks, TOK_SUB * TOP)
    onehot = (chosen[:, :, None] == jnp.arange(EXPERTS, dtype=jnp.int32)[None, None, :]).astype(jnp.int32)
    before = jnp.cumsum(onehot, axis=1) - onehot
    slot_index = lax.optimization_barrier(jnp.sum(before * onehot, axis=2)).astype(jnp.int32)
    block_index = jnp.arange(blocks, dtype=jnp.int32)[:, None]
    target = ((chosen * blocks + block_index) * CAPS + slot_index).reshape(-1).astype(jnp.int32)
    repeated = jnp.repeat(hidden_in, TOP, axis=0)
    buffer = jnp.zeros((EXPERTS * blocks * CAPS, D), jnp.bfloat16).at[target].set(repeated)
    buffer = buffer.reshape(EXPERTS, blocks * CAPS, D)

    def expert(packed):
        inputs, gate_matrix, up_matrix, down_matrix = packed
        gate_act = times_rows(inputs, gate_matrix)
        up_act = times_rows(inputs, up_matrix)
        activated = (jax.nn.silu(gate_act) * up_act).astype(jnp.bfloat16)
        groups_act = activated.reshape(inputs.shape[0], N_SEQ, HID_DEV).transpose(1, 0, 2)
        groups_down = down_matrix.reshape(N_SEQ, HID_DEV, D)

        def add_group(total, pair):
            part, down_rows = pair
            term = rounded(jnp.dot(part, down_rows, preferred_element_type=jnp.float32)).astype(jnp.float32)
            return (total + term, None)
        total, unused = lax.scan(add_group, jnp.zeros((inputs.shape[0], D), jnp.float32), (groups_act, groups_down))
        return total.astype(jnp.bfloat16)
    outputs = lax.map(expert, (buffer, w_gate, w_up, w_down)).reshape(-1, D)
    picked = outputs[target].astype(jnp.float32).reshape(TOKENS, TOP, D)
    mixed = hidden_in.astype(jnp.float32) + lax.optimization_barrier(jnp.sum(gate_values[:, :, None] * picked, axis=1))
    return mixed.astype(jnp.bfloat16)
```

```python
import functools

import jax
import jax.numpy as jnp
from jax import lax
from jax.experimental import pallas as pl
from jax.experimental.pallas import tpu as pltpu
from jax.sharding import PartitionSpec as P

HD = 128
TOP = 2


def entering(array, axis, combine, identity):
    devices, place = (lax.axis_size(axis), lax.axis_index(axis))
    everything = lax.all_gather(array.astype(jnp.bfloat16), axis)
    start = jnp.broadcast_to(jnp.asarray(identity, array.dtype), array.shape)

    def hop(k, before):
        reached = k < place
        new = combine(before, everything[k].astype(array.dtype))
        return jnp.where(reached, new, before)

    return lax.fori_loop(0, devices, hop, start)


def features(x):
    widened = x.astype(jnp.float32)
    return (widened * jax.nn.sigmoid(widened)).astype(jnp.bfloat16)


def times_rows(left, right):
    return lax.dot_general(
        left, right, (((1,), (1,)), ((), ())), preferred_element_type=jnp.float32
    )


def local(
    query_proj,
    key_proj,
    value_proj,
    residual,
    out_weight,
    expert_ids,
    gate_values,
    w_gate,
    w_up,
    w_down,
):
    tokens_here = query_proj.shape[0]
    heads_here = query_proj.shape[1] // HD
    query_feat = features(query_proj).reshape(tokens_here, heads_here, HD)
    key_feat = features(key_proj).reshape(tokens_here, heads_here, HD)
    value_rows = value_proj.reshape(tokens_here, heads_here, HD)
    span_state = jnp.einsum(
        "thd,the->hde", key_feat, value_rows, preferred_element_type=jnp.float32
    )
    earlier = entering(span_state, "seq", lambda a, b: a + b, jnp.zeros_like(span_state))
    prefix = earlier.astype(jnp.bfloat16)
    earlier_term = jnp.einsum(
        "thd,hde->the", query_feat, prefix, preferred_element_type=jnp.float32
    )
    scores = jnp.einsum("thd,shd->hts", query_feat, key_feat, preferred_element_type=jnp.float32)
    causal = jnp.arange(tokens_here)[:, None] >= jnp.arange(tokens_here)[None, :]
    weights = jnp.where(causal[None], scores, 0.0).astype(jnp.bfloat16)
    local_term = jnp.einsum("hts,she->the", weights, value_rows, preferred_element_type=jnp.float32)
    combined = local_term + earlier_term
    normed = combined * lax.rsqrt(jnp.mean(combined * combined, axis=-1, keepdims=True) + 1e-06)
    normed = normed.astype(jnp.bfloat16).reshape(tokens_here, heads_here * HD)
    partial_out = times_rows(normed, lax.all_gather(out_weight, "seq", axis=0, tiled=True))
    summed = lax.psum_scatter(
        partial_out.astype(jnp.bfloat16), "exp", scatter_dimension=0, tiled=True
    ).astype(jnp.float32)
    mixed_in = (residual.astype(jnp.float32) + summed).astype(jnp.bfloat16)
    groups = lax.axis_size("exp")
    tok_sub = residual.shape[0]
    capacity = max(2, (3 * tok_sub * TOP + 2 * groups - 1) // (2 * groups))
    local_rows = groups * capacity
    chosen = expert_ids.reshape(-1)
    onehot = (chosen[:, None] == jnp.arange(groups, dtype=jnp.int32)[None, :]).astype(jnp.int32)
    place = jnp.arange(tok_sub * TOP)
    before = jnp.sum((place[:, None] > place[None, :])[:, :, None] * onehot[None], axis=1)
    slot_index = jnp.sum(before * onehot, axis=1)
    target = chosen * capacity + slot_index
    targets = target.reshape(tok_sub, TOP)
    slot_ids = jnp.arange(local_rows, dtype=jnp.int32)
    placing = jnp.any(slot_ids[:, None, None] == targets[None, :, :], axis=2).astype(jnp.bfloat16)
    outgoing = jnp.dot(placing, mixed_in, preferred_element_type=jnp.float32).astype(jnp.bfloat16)
    outgoing = outgoing.reshape(groups, capacity, -1)
    gate_local = w_gate[0]
    up_local = w_up[0]
    down_local = w_down[0]
    hidden_here = gate_local.shape[0]
    arrived = lax.all_to_all(outgoing, "exp", split_axis=0, concat_axis=0, tiled=True).reshape(
        local_rows, -1
    )
    rows_part = lax.all_gather(arrived, "seq", axis=0, tiled=True)
    acts = jnp.concatenate(
        [times_rows(rows_part, gate_local), times_rows(rows_part, up_local)], axis=1
    )
    gate_act = acts[:, :hidden_here]
    up_act = acts[:, hidden_here:]
    activated = (jax.nn.silu(gate_act) * up_act).astype(jnp.bfloat16)
    rows_part = activated
    expert_sums = lax.psum_scatter(
        jnp.dot(rows_part, down_local, preferred_element_type=jnp.float32).astype(jnp.bfloat16),
        "seq",
        scatter_dimension=0,
        tiled=True,
    )
    expert_out = expert_sums.reshape(groups, capacity, -1)
    returned = lax.all_to_all(expert_out, "exp", split_axis=0, concat_axis=0, tiled=True).reshape(
        local_rows, -1
    )
    picked = returned[target].astype(jnp.float32).reshape(tok_sub, TOP, -1)
    mixed = mixed_in.astype(jnp.float32) + jnp.sum(gate_values[:, :, None] * picked, axis=1)
    return mixed.astype(jnp.bfloat16)


MESH = pl.DeviceIdType.MESH
VMEM = pltpu.VMEM


def _place(ref, kind, size, i):
    if kind == "row":
        return ref.at[pl.ds(pl.multiple_of(i * size, size), size), :]
    if kind == "col":
        return ref.at[:, pl.ds(pl.multiple_of(i * size, size), size)]
    return ref


def _greet(axis, peers):
    barrier = pltpu.get_barrier_semaphore()
    for peer in peers:
        pl.semaphore_signal(barrier, inc=1, device_id={axis: peer}, device_id_type=MESH)
    pl.semaphore_wait(barrier, len(peers))


def _exchange_kernel(axis, n, kinds, *refs):
    m = len(kinds)
    ins, outs = refs[:m], refs[m : 2 * m]
    send, recv, own = refs[2 * m :]
    me = lax.axis_index(axis)
    peers = [lax.rem(me + k, n) for k in range(1, n)]
    _greet(axis, peers)
    copies = []
    for k, peer in enumerate(peers):
        for a, (sk, ss, dk, ds) in enumerate(kinds):
            c = pltpu.make_async_remote_copy(
                src_ref=_place(ins[a], sk, ss, peer),
                dst_ref=_place(outs[a], dk, ds, me),
                send_sem=send.at[a, k],
                recv_sem=recv.at[a, k],
                device_id={axis: peer},
                device_id_type=MESH,
            )
            c.start()
            copies.append(c)
    for a, (sk, ss, dk, ds) in enumerate(kinds):
        c = pltpu.make_async_copy(
            _place(ins[a], sk, ss, me), _place(outs[a], dk, ds, me), own.at[a]
        )
        c.start()
        copies.append(c)
    for c in copies:
        c.wait()


def exchange(axis, kinds, ins, out_shapes, cid):
    n, m = lax.axis_size(axis), len(ins)
    return pl.pallas_call(
        functools.partial(_exchange_kernel, axis, n, kinds),
        out_shape=out_shapes,
        in_specs=[pl.BlockSpec(memory_space=VMEM)] * m,
        out_specs=[pl.BlockSpec(memory_space=VMEM)] * m,
        scratch_shapes=[
            pltpu.SemaphoreType.DMA((m, n - 1)),
            pltpu.SemaphoreType.DMA((m, n - 1)),
            pltpu.SemaphoreType.DMA((m,)),
        ],
        compiler_params=pltpu.CompilerParams(
            collective_id=cid, has_side_effects=True, vmem_limit_bytes=32 << 20
        ),
    )(*ins)


def _around(s):
    c, x, y = lax.rem(s, 2), lax.rem(s // 2, 2), s // 4
    right = s + 2 - 4 * x
    up = s + 4 - 8 * y
    return right, up, up + 2 - 4 * x, 1 - 2 * c


def _gather_kernel(rows, width, in_ref, out_ref, send, recv, own):
    s = lax.axis_index("seq")
    sx, sy, sd, flip = _around(s)
    sib = s + flip
    half = rows // 2

    def at(i, part=None):
        cols = pl.ds(pl.multiple_of(i * width, width), width)
        if part is None:
            return out_ref.at[:, cols]
        return out_ref.at[pl.ds(part * half, half), cols]

    def push(src, dst, to, k):
        c = pltpu.make_async_remote_copy(
            src_ref=src, dst_ref=dst, send_sem=send.at[k], recv_sem=recv.at[k],
            device_id={"seq": to}, device_id_type=MESH,
        )
        c.start()
        return c

    _greet("seq", [sx, sy, sib])
    to_x = push(in_ref, at(s), sx, 0)
    to_y = push(in_ref, at(s), sy, 1)
    to_s = push(in_ref, at(s), sib, 2)
    mine = pltpu.make_async_copy(in_ref, at(s), own)
    mine.start()
    to_x.wait_recv()
    fy = push(at(sx, 0), at(sx, 0), sy, 3)
    gx = push(at(sx), at(sx), sib, 4)
    to_y.wait_recv()
    fx = push(at(sy, 1), at(sy, 1), sx, 5)
    gy = push(at(sy), at(sy), sib, 6)
    fy.wait_recv()
    fx.wait_recv()
    gd = push(at(sd), at(sd), sib, 7)
    to_s.wait_recv()
    gx.wait_recv()
    gy.wait_recv()
    gd.wait_recv()
    for c in (to_x, to_y, to_s, fy, gx, fx, gy, gd):
        c.wait_send()
    mine.wait()


def gather_columns(x, cid):
    rows, width = x.shape
    n = lax.axis_size("seq")
    return pl.pallas_call(
        functools.partial(_gather_kernel, rows, width),
        out_shape=jax.ShapeDtypeStruct((rows, n * width), x.dtype),
        in_specs=[pl.BlockSpec(memory_space=VMEM)],
        out_specs=pl.BlockSpec(memory_space=VMEM),
        scratch_shapes=[
            pltpu.SemaphoreType.DMA((8,)),
            pltpu.SemaphoreType.DMA((8,)),
            pltpu.SemaphoreType.DMA,
        ],
        compiler_params=pltpu.CompilerParams(
            collective_id=cid, has_side_effects=True, vmem_limit_bytes=32 << 20
        ),
    )(x)


def _scatter_kernel(rows, width, in_ref, out_ref, rs, st, rd, rx, ry, send, recv):
    s = lax.axis_index("seq")
    sx, sy, sd, flip = _around(s)
    sib = s + flip
    half = rows // 2
    step = 32

    def part(i):
        return in_ref.at[:, pl.ds(pl.multiple_of(i * width, width), width)]

    def push(src, dst, to, k):
        c = pltpu.make_async_remote_copy(
            src_ref=src, dst_ref=dst, send_sem=send.at[k], recv_sem=recv.at[k],
            device_id={"seq": to}, device_id_type=MESH,
        )
        c.start()
        return c

    def add(dst, d0, count, terms):
        @pl.loop(0, count // step)
        def _(i):
            total = None
            for ref, base in terms:
                v = ref[pl.ds(pl.multiple_of(base + i * step, step), step), :].astype(jnp.float32)
                total = v if total is None else total + v
            dst[pl.ds(pl.multiple_of(d0 + i * step, step), step), :] = total.astype(dst.dtype)

    def top(ref):
        return ref.at[pl.ds(0, half), :]

    def bottom(ref):
        return ref.at[pl.ds(half, half), :]

    _greet("seq", [sx, sy, sib])
    cs = [push(part(i + flip), rs.at[k], sib, k) for k, i in enumerate((sd, sx, sy, s))]
    cs[0].wait_recv()
    add(st.at[0], 0, rows, [(part(sd), 0), (rs.at[0], 0)])
    dt = push(top(st.at[0]), rd.at[0], sx, 4)
    db = push(bottom(st.at[0]), rd.at[1], sy, 5)
    cs[1].wait_recv()
    add(st.at[1], 0, rows, [(part(sx), 0), (rs.at[1], 0)])
    xt = push(top(st.at[1]), top(rx), sx, 6)
    cs[2].wait_recv()
    add(st.at[2], 0, rows, [(part(sy), 0), (rs.at[2], 0)])
    yb = push(bottom(st.at[2]), bottom(ry), sy, 7)
    cs[3].wait_recv()
    dt.wait_recv()
    add(st.at[2], 0, half, [(st.at[2], 0), (rd.at[0], 0)])
    yt = push(top(st.at[2]), top(ry), sy, 8)
    db.wait_recv()
    add(st.at[1], half, half, [(st.at[1], half), (rd.at[1], 0)])
    xb = push(bottom(st.at[1]), bottom(rx), sx, 9)
    xt.wait_recv()
    yt.wait_recv()
    add(out_ref, 0, half, [(part(s), 0), (rs.at[3], 0), (rx, 0), (ry, 0)])
    yb.wait_recv()
    xb.wait_recv()
    add(out_ref, half, half, [(part(s), half), (rs.at[3], half), (rx, half), (ry, half)])
    for c in (*cs, dt, db, xt, yb, yt, xb):
        c.wait_send()


def scatter_columns(x, cid):
    rows, whole = x.shape
    width = whole // lax.axis_size("seq")
    b = x.dtype
    return pl.pallas_call(
        functools.partial(_scatter_kernel, rows, width),
        out_shape=jax.ShapeDtypeStruct((rows, width), b),
        in_specs=[pl.BlockSpec(memory_space=VMEM)],
        out_specs=pl.BlockSpec(memory_space=VMEM),
        scratch_shapes=[
            VMEM((4, rows, width), b),
            VMEM((3, rows, width), b),
            VMEM((2, rows // 2, width), b),
            VMEM((rows, width), b),
            VMEM((rows, width), b),
            pltpu.SemaphoreType.DMA((10,)),
            pltpu.SemaphoreType.DMA((10,)),
        ],
        compiler_params=pltpu.CompilerParams(
            collective_id=cid, has_side_effects=True, vmem_limit_bytes=40 << 20
        ),
    )(x)


def by_heads(
    query_proj,
    key_proj,
    value_proj,
    residual,
    out_weight,
    expert_ids,
    gate_values,
    w_gate,
    w_up,
    w_down,
):
    n_seq, groups = lax.axis_size("seq"), lax.axis_size("exp")
    block = query_proj.shape[0]
    tokens = n_seq * block
    tok_sub = residual.shape[0]
    width = residual.shape[1] // n_seq
    plane = n_seq * tok_sub
    capacity = max(2, (3 * tok_sub * TOP + 2 * groups - 1) // (2 * groups))
    bf, f32 = jnp.bfloat16, jnp.float32
    meta = jnp.concatenate(
        [expert_ids.T.astype(f32), gate_values.T, jnp.zeros((8 - 2 * TOP, tok_sub), f32)], axis=0
    )
    meta = jnp.pad(meta, ((0, 0), (0, 128 - tok_sub)))
    head = ("col", HD, "row", block)
    q, k, v, res, meta = exchange(
        "seq",
        (head, head, head, ("col", width, "row", tok_sub), ("all", 0, "row", 8)),
        (query_proj, key_proj, value_proj, residual, meta),
        [jax.ShapeDtypeStruct((tokens, HD), bf)] * 3
        + [jax.ShapeDtypeStruct((plane, width), bf), jax.ShapeDtypeStruct((8 * n_seq, 128), f32)],
        0,
    )
    qf = features(q).reshape(n_seq, block, HD)
    kf = features(k).reshape(n_seq, block, HD)
    vr = v.reshape(n_seq, block, HD)
    states = jnp.einsum("btd,bte->bde", kf, vr, preferred_element_type=f32)
    running, before_it = jnp.zeros_like(states[0]), []
    for b in range(n_seq):
        before_it.append(running)
        running = running + states[b]
    prefix = jnp.stack(before_it).astype(bf)
    scores = jnp.einsum("btd,bsd->bts", qf, kf, preferred_element_type=f32)
    causal = jnp.arange(block)[:, None] >= jnp.arange(block)[None, :]
    weights = jnp.where(causal[None], scores, 0.0).astype(bf)
    combined = jnp.einsum("bts,bse->bte", weights, vr, preferred_element_type=f32)
    combined = combined + jnp.einsum("btd,bde->bte", qf, prefix, preferred_element_type=f32)
    normed = combined * lax.rsqrt(jnp.mean(combined * combined, axis=-1, keepdims=True) + 1e-06)
    normed = normed.astype(bf).reshape(n_seq, groups, tok_sub, HD)
    normed = normed.transpose(1, 0, 2, 3).reshape(tokens, HD)

    partial_out = times_rows(gather_columns(normed, 1), out_weight).astype(bf)
    (parts,) = exchange(
        "exp",
        (("row", plane, "row", plane),),
        (partial_out,),
        [jax.ShapeDtypeStruct((tokens, width), bf)],
        2,
    )
    summed = jnp.sum(parts.reshape(groups, plane, width).astype(f32), axis=0)
    mixed_in = (res.astype(f32) + summed).astype(bf)

    meta = meta.reshape(n_seq, 8, 128)
    ids = meta[:, :TOP, :tok_sub].astype(jnp.int32).transpose(0, 2, 1)
    gates = meta[:, TOP : 2 * TOP, :tok_sub].transpose(0, 2, 1).reshape(plane, TOP)
    chosen = ids.reshape(n_seq, tok_sub * TOP)
    onehot = (chosen[:, :, None] == jnp.arange(groups, dtype=jnp.int32)).astype(jnp.int32)
    earlier = (jnp.arange(tok_sub * TOP)[:, None] > jnp.arange(tok_sub * TOP)[None, :])
    before = jnp.sum(earlier[None, :, :, None] * onehot[:, None, :, :], axis=2)
    slot = jnp.sum(before * onehot, axis=2)
    target = (chosen * n_seq + jnp.arange(n_seq, dtype=jnp.int32)[:, None]) * capacity + slot
    target = target.reshape(plane, TOP)
    slots = jnp.arange(groups * n_seq * capacity, dtype=jnp.int32)
    picks = [(target[:, j : j + 1] == slots[None, :]).astype(bf) for j in range(TOP)]
    placing = picks[0]
    for p in picks[1:]:
        placing = placing + p
    outgoing = lax.dot_general(
        placing, mixed_in, (((0,), (0,)), ((), ())), preferred_element_type=f32
    ).astype(bf)
    load = n_seq * capacity
    rows_shape = [jax.ShapeDtypeStruct((groups * load, width), bf)]
    (arrived,) = exchange("exp", (("row", load, "row", load),), (outgoing,), rows_shape, 3)
    rows = gather_columns(arrived, 4)
    gate_act = times_rows(rows, w_gate[0])
    up_act = times_rows(rows, w_up[0])
    activated = (jax.nn.silu(gate_act) * up_act).astype(bf)
    down = jnp.dot(activated, w_down[0], preferred_element_type=f32).astype(bf)
    sums = scatter_columns(down, 5)
    (returned,) = exchange("exp", (("row", load, "row", load),), (sums,), rows_shape, 6)
    mixed = mixed_in.astype(f32)
    extra = jnp.zeros_like(mixed)
    for j in range(TOP):
        picked = jnp.dot(picks[j], returned, preferred_element_type=f32)
        extra = extra + gates[:, j : j + 1] * picked
    mixed = (mixed + extra).astype(bf)
    (out,) = exchange(
        "seq",
        (("row", tok_sub, "col", width),),
        (mixed,),
        [jax.ShapeDtypeStruct(residual.shape, bf)],
        7,
    )
    return out


def solution(mesh):
    return jax.shard_map(
        by_heads if mesh.shape["seq"] == 8 and mesh.shape["exp"] == 4 else local,
        mesh=mesh,
        in_specs=(
            P("seq", "exp"),
            P("seq", "exp"),
            P("seq", "exp"),
            P(("seq", "exp"), None),
            P("seq", "exp"),
            P(("seq", "exp"), None),
            P(("seq", "exp"), None),
            P("exp", "seq", None),
            P("exp", "seq", None),
            P("exp", "seq", None),
        ),
        out_specs=P(("seq", "exp"), None),
        check_vma=False,
    )
```

```python
import functools

import jax
import jax.numpy as jnp
from jax import lax
from jax.experimental import pallas as pl
from jax.experimental.pallas import tpu as pltpu
from jax.sharding import PartitionSpec as P

HD = 128
TOP = 2


def entering(array, axis, combine, identity):
    devices, place = (lax.axis_size(axis), lax.axis_index(axis))
    everything = lax.all_gather(array.astype(jnp.bfloat16), axis)
    start = jnp.broadcast_to(jnp.asarray(identity, array.dtype), array.shape)

    def hop(k, before):
        reached = k < place
        new = combine(before, everything[k].astype(array.dtype))
        return jnp.where(reached, new, before)

    return lax.fori_loop(0, devices, hop, start)


def features(x):
    widened = x.astype(jnp.float32)
    return (widened * jax.nn.sigmoid(widened)).astype(jnp.bfloat16)


def times_rows(left, right):
    return lax.dot_general(
        left, right, (((1,), (1,)), ((), ())), preferred_element_type=jnp.float32
    )


def local(
    query_proj,
    key_proj,
    value_proj,
    residual,
    out_weight,
    expert_ids,
    gate_values,
    w_gate,
    w_up,
    w_down,
):
    tokens_here = query_proj.shape[0]
    heads_here = query_proj.shape[1] // HD
    query_feat = features(query_proj).reshape(tokens_here, heads_here, HD)
    key_feat = features(key_proj).reshape(tokens_here, heads_here, HD)
    value_rows = value_proj.reshape(tokens_here, heads_here, HD)
    span_state = jnp.einsum(
        "thd,the->hde", key_feat, value_rows, preferred_element_type=jnp.float32
    )
    earlier = entering(span_state, "seq", lambda a, b: a + b, jnp.zeros_like(span_state))
    prefix = earlier.astype(jnp.bfloat16)
    earlier_term = jnp.einsum(
        "thd,hde->the", query_feat, prefix, preferred_element_type=jnp.float32
    )
    scores = jnp.einsum("thd,shd->hts", query_feat, key_feat, preferred_element_type=jnp.float32)
    causal = jnp.arange(tokens_here)[:, None] >= jnp.arange(tokens_here)[None, :]
    weights = jnp.where(causal[None], scores, 0.0).astype(jnp.bfloat16)
    local_term = jnp.einsum("hts,she->the", weights, value_rows, preferred_element_type=jnp.float32)
    combined = local_term + earlier_term
    normed = combined * lax.rsqrt(jnp.mean(combined * combined, axis=-1, keepdims=True) + 1e-06)
    normed = normed.astype(jnp.bfloat16).reshape(tokens_here, heads_here * HD)
    partial_out = times_rows(normed, lax.all_gather(out_weight, "seq", axis=0, tiled=True))
    summed = lax.psum_scatter(
        partial_out.astype(jnp.bfloat16), "exp", scatter_dimension=0, tiled=True
    ).astype(jnp.float32)
    mixed_in = (residual.astype(jnp.float32) + summed).astype(jnp.bfloat16)
    groups = lax.axis_size("exp")
    tok_sub = residual.shape[0]
    capacity = max(2, (3 * tok_sub * TOP + 2 * groups - 1) // (2 * groups))
    local_rows = groups * capacity
    chosen = expert_ids.reshape(-1)
    onehot = (chosen[:, None] == jnp.arange(groups, dtype=jnp.int32)[None, :]).astype(jnp.int32)
    place = jnp.arange(tok_sub * TOP)
    before = jnp.sum((place[:, None] > place[None, :])[:, :, None] * onehot[None], axis=1)
    slot_index = jnp.sum(before * onehot, axis=1)
    target = chosen * capacity + slot_index
    targets = target.reshape(tok_sub, TOP)
    slot_ids = jnp.arange(local_rows, dtype=jnp.int32)
    placing = jnp.any(slot_ids[:, None, None] == targets[None, :, :], axis=2).astype(jnp.bfloat16)
    outgoing = jnp.dot(placing, mixed_in, preferred_element_type=jnp.float32).astype(jnp.bfloat16)
    outgoing = outgoing.reshape(groups, capacity, -1)
    gate_local = w_gate[0]
    up_local = w_up[0]
    down_local = w_down[0]
    hidden_here = gate_local.shape[0]
    arrived = lax.all_to_all(outgoing, "exp", split_axis=0, concat_axis=0, tiled=True).reshape(
        local_rows, -1
    )
    rows_part = lax.all_gather(arrived, "seq", axis=0, tiled=True)
    acts = jnp.concatenate(
        [times_rows(rows_part, gate_local), times_rows(rows_part, up_local)], axis=1
    )
    gate_act = acts[:, :hidden_here]
    up_act = acts[:, hidden_here:]
    activated = (jax.nn.silu(gate_act) * up_act).astype(jnp.bfloat16)
    rows_part = activated
    expert_sums = lax.psum_scatter(
        jnp.dot(rows_part, down_local, preferred_element_type=jnp.float32).astype(jnp.bfloat16),
        "seq",
        scatter_dimension=0,
        tiled=True,
    )
    expert_out = expert_sums.reshape(groups, capacity, -1)
    returned = lax.all_to_all(expert_out, "exp", split_axis=0, concat_axis=0, tiled=True).reshape(
        local_rows, -1
    )
    picked = returned[target].astype(jnp.float32).reshape(tok_sub, TOP, -1)
    mixed = mixed_in.astype(jnp.float32) + jnp.sum(gate_values[:, :, None] * picked, axis=1)
    return mixed.astype(jnp.bfloat16)


MESH = pl.DeviceIdType.MESH
VMEM = pltpu.VMEM


def _place(ref, kind, size, i):
    if kind == "row":
        return ref.at[pl.ds(pl.multiple_of(i * size, size), size), :]
    if kind == "col":
        return ref.at[:, pl.ds(pl.multiple_of(i * size, size), size)]
    return ref


def _greet(axis, peers):
    barrier = pltpu.get_barrier_semaphore()
    for peer in peers:
        pl.semaphore_signal(barrier, inc=1, device_id={axis: peer}, device_id_type=MESH)
    pl.semaphore_wait(barrier, len(peers))


def _exchange_kernel(axis, n, kinds, *refs):
    m = len(kinds)
    ins, outs = refs[:m], refs[m : 2 * m]
    send, recv, own = refs[2 * m :]
    me = lax.axis_index(axis)
    peers = [lax.rem(me + k, n) for k in range(1, n)]
    _greet(axis, peers)
    copies = []
    for k, peer in enumerate(peers):
        for a, (sk, ss, dk, ds) in enumerate(kinds):
            c = pltpu.make_async_remote_copy(
                src_ref=_place(ins[a], sk, ss, peer),
                dst_ref=_place(outs[a], dk, ds, me),
                send_sem=send.at[a, k],
                recv_sem=recv.at[a, k],
                device_id={axis: peer},
                device_id_type=MESH,
            )
            c.start()
            copies.append(c)
    for a, (sk, ss, dk, ds) in enumerate(kinds):
        c = pltpu.make_async_copy(
            _place(ins[a], sk, ss, me), _place(outs[a], dk, ds, me), own.at[a]
        )
        c.start()
        copies.append(c)
    for c in copies:
        c.wait()


def exchange(axis, kinds, ins, out_shapes, cid):
    n, m = lax.axis_size(axis), len(ins)
    return pl.pallas_call(
        functools.partial(_exchange_kernel, axis, n, kinds),
        out_shape=out_shapes,
        in_specs=[pl.BlockSpec(memory_space=VMEM)] * m,
        out_specs=[pl.BlockSpec(memory_space=VMEM)] * m,
        scratch_shapes=[
            pltpu.SemaphoreType.DMA((m, n - 1)),
            pltpu.SemaphoreType.DMA((m, n - 1)),
            pltpu.SemaphoreType.DMA((m,)),
        ],
        compiler_params=pltpu.CompilerParams(
            collective_id=cid, has_side_effects=True, vmem_limit_bytes=32 << 20
        ),
    )(*ins)


def _around(s):
    c, x, y = lax.rem(s, 2), lax.rem(s // 2, 2), s // 4
    right = s + 2 - 4 * x
    up = s + 4 - 8 * y
    return right, up, up + 2 - 4 * x, 1 - 2 * c


def _gather_kernel(rows, width, in_ref, out_ref, send, recv, own):
    s = lax.axis_index("seq")
    sx, sy, sd, flip = _around(s)
    sib = s + flip
    half = rows // 2

    def at(i, part=None):
        cols = pl.ds(pl.multiple_of(i * width, width), width)
        if part is None:
            return out_ref.at[:, cols]
        return out_ref.at[pl.ds(part * half, half), cols]

    def push(src, dst, to, k):
        c = pltpu.make_async_remote_copy(
            src_ref=src, dst_ref=dst, send_sem=send.at[k], recv_sem=recv.at[k],
            device_id={"seq": to}, device_id_type=MESH,
        )
        c.start()
        return c

    _greet("seq", [sx, sy, sib])
    to_x = push(in_ref, at(s), sx, 0)
    to_y = push(in_ref, at(s), sy, 1)
    to_s = push(in_ref, at(s), sib, 2)
    mine = pltpu.make_async_copy(in_ref, at(s), own)
    mine.start()
    to_x.wait_recv()
    fy = push(at(sx, 0), at(sx, 0), sy, 3)
    gx = push(at(sx), at(sx), sib, 4)
    to_y.wait_recv()
    fx = push(at(sy, 1), at(sy, 1), sx, 5)
    gy = push(at(sy), at(sy), sib, 6)
    fy.wait_recv()
    fx.wait_recv()
    gd = push(at(sd), at(sd), sib, 7)
    to_s.wait_recv()
    gx.wait_recv()
    gy.wait_recv()
    gd.wait_recv()
    for c in (to_x, to_y, to_s, fy, gx, fx, gy, gd):
        c.wait_send()
    mine.wait()


def gather_columns(x, cid):
    rows, width = x.shape
    n = lax.axis_size("seq")
    return pl.pallas_call(
        functools.partial(_gather_kernel, rows, width),
        out_shape=jax.ShapeDtypeStruct((rows, n * width), x.dtype),
        in_specs=[pl.BlockSpec(memory_space=VMEM)],
        out_specs=pl.BlockSpec(memory_space=VMEM),
        scratch_shapes=[
            pltpu.SemaphoreType.DMA((8,)),
            pltpu.SemaphoreType.DMA((8,)),
            pltpu.SemaphoreType.DMA,
        ],
        compiler_params=pltpu.CompilerParams(
            collective_id=cid, has_side_effects=True, vmem_limit_bytes=32 << 20
        ),
    )(x)


def _pusher(send, recv):
    def push(src, dst, to, k):
        c = pltpu.make_async_remote_copy(
            src_ref=src, dst_ref=dst, send_sem=send.at[k], recv_sem=recv.at[k],
            device_id={"seq": to}, device_id_type=MESH,
        )
        c.start()
        return c

    return push


def _up_kernel(
    rows, width, tile, in_ref, gate_hbm, up_hbm, out_ref, all_rows, acc, held, wsem, send, recv, own
):
    s = lax.axis_index("seq")
    sx, sy, sd, flip = _around(s)
    sib = s + flip
    half = rows // 2
    pair = 2 * width
    hidden = out_ref.shape[1]
    chips = [i // 2 for i in (s, sx, sy, sd)]
    loads = []
    for k, chip in enumerate(chips):
        for m, hbm in enumerate((gate_hbm, up_hbm)):
            c = pltpu.make_async_copy(
                hbm.at[0, :, pl.ds(pl.multiple_of(chip * pair, pair), pair)],
                held.at[k, m],
                wsem.at[k, m],
            )
            c.start()
            loads.append(c)
    push = _pusher(send, recv)

    def at(i, part=None):
        cols = pl.ds(pl.multiple_of(i * width, width), width)
        if part is None:
            return all_rows.at[:, cols]
        return all_rows.at[pl.ds(part * half, half), cols]

    def multiply(k):
        loads[2 * k].wait()
        loads[2 * k + 1].wait()
        left = pl.ds(pl.multiple_of(chips[k] * pair, pair), pair)

        @pl.loop(0, hidden // tile)
        def _(j):
            at_j = pl.ds(pl.multiple_of(j * tile, tile), tile)
            x = all_rows[:, left]
            g = times_rows(x, held[k, 0, at_j, :])
            u = times_rows(x, held[k, 1, at_j, :])
            if k:
                g = g + acc[0, :, at_j]
                u = u + acc[1, :, at_j]
            if k < 3:
                acc[0, :, at_j] = g
                acc[1, :, at_j] = u
            else:
                out_ref[:, at_j] = (g / (1.0 + jnp.exp(-g)) * u).astype(out_ref.dtype)

    _greet("seq", [sx, sy, sib])
    to_x = push(in_ref, at(s), sx, 0)
    to_y = push(in_ref, at(s), sy, 1)
    to_s = push(in_ref, at(s), sib, 2)
    mine = pltpu.make_async_copy(in_ref, at(s), own)
    mine.start()
    to_x.wait_recv()
    fy = push(at(sx, 0), at(sx, 0), sy, 3)
    gx = push(at(sx), at(sx), sib, 4)
    to_y.wait_recv()
    fx = push(at(sy, 1), at(sy, 1), sx, 5)
    gy = push(at(sy), at(sy), sib, 6)
    mine.wait()
    to_s.wait_recv()
    multiply(0)
    gx.wait_recv()
    multiply(1)
    gy.wait_recv()
    multiply(2)
    fy.wait_recv()
    fx.wait_recv()
    gd = push(at(sd), at(sd), sib, 7)
    gd.wait_recv()
    multiply(3)
    for c in (to_x, to_y, to_s, fy, gx, fx, gy, gd):
        c.wait_send()


def gathered_up(x, w_gate, w_up, cid):
    rows, width = x.shape
    hidden = w_gate.shape[1]
    n = lax.axis_size("seq")
    return pl.pallas_call(
        functools.partial(_up_kernel, rows, width, 384),
        out_shape=jax.ShapeDtypeStruct((rows, hidden), x.dtype),
        in_specs=[pl.BlockSpec(memory_space=VMEM)] + [pl.BlockSpec(memory_space=pl.ANY)] * 2,
        out_specs=pl.BlockSpec(memory_space=VMEM),
        scratch_shapes=[
            VMEM((rows, n * width), x.dtype),
            VMEM((2, rows, hidden), jnp.float32),
            VMEM((4, 2, hidden, 2 * width), x.dtype),
            pltpu.SemaphoreType.DMA((4, 2)),
            pltpu.SemaphoreType.DMA((8,)),
            pltpu.SemaphoreType.DMA((8,)),
            pltpu.SemaphoreType.DMA,
        ],
        compiler_params=pltpu.CompilerParams(
            collective_id=cid, has_side_effects=True, vmem_limit_bytes=52 << 20
        ),
    )(x, w_gate, w_up)


def _down_kernel(
    rows, width, tile, in_ref, down_hbm, out_ref, held, sb, rs, st, so, rd, rx, ry, wsem, send, recv
):
    s = lax.axis_index("seq")
    sx, sy, sd, flip = _around(s)
    sib = s + flip
    half = rows // 2
    step = 32
    order = [sd + flip, sx + flip, sy + flip, sd, sx, sy, s + flip, s]
    loads = []
    for k, i in enumerate(order):
        c = pltpu.make_async_copy(
            down_hbm.at[0, :, pl.ds(pl.multiple_of(i * width, width), width)],
            held.at[k],
            wsem.at[k],
        )
        c.start()
        loads.append(c)
    push = _pusher(send, recv)

    def product(k, dst, more=None):
        loads[k].wait()

        @pl.loop(0, width // tile)
        def _(j):
            at_j = pl.ds(pl.multiple_of(j * tile, tile), tile)
            r = jnp.dot(in_ref[...], held[k, :, at_j], preferred_element_type=jnp.float32)
            if more is not None:
                r = r + more[:, at_j].astype(jnp.float32)
            dst[:, at_j] = r.astype(dst.dtype)

    def add(dst, d0, count, terms):
        @pl.loop(0, count // step)
        def _(i):
            total = None
            for ref, base in terms:
                v = ref[pl.ds(pl.multiple_of(base + i * step, step), step), :].astype(jnp.float32)
                total = v if total is None else total + v
            dst[pl.ds(pl.multiple_of(d0 + i * step, step), step), :] = total.astype(dst.dtype)

    def top(ref):
        return ref.at[pl.ds(0, half), :]

    def bottom(ref):
        return ref.at[pl.ds(half, half), :]

    _greet("seq", [sx, sy, sib])
    cs = []
    for k in range(3):
        product(k, sb.at[k])
        cs.append(push(sb.at[k], rs.at[k], sib, k))
    cs[0].wait_recv()
    product(3, st.at[0], rs.at[0])
    dt = push(top(st.at[0]), rd.at[0], sx, 4)
    db = push(bottom(st.at[0]), rd.at[1], sy, 5)
    cs[1].wait_recv()
    product(4, st.at[1], rs.at[1])
    xt = push(top(st.at[1]), top(rx), sx, 6)
    cs[2].wait_recv()
    product(5, st.at[2], rs.at[2])
    yb = push(bottom(st.at[2]), bottom(ry), sy, 7)
    product(6, sb.at[3])
    cs.append(push(sb.at[3], rs.at[3], sib, 3))
    dt.wait_recv()
    add(st.at[2], 0, half, [(st.at[2], 0), (rd.at[0], 0)])
    yt = push(top(st.at[2]), top(ry), sy, 8)
    db.wait_recv()
    add(st.at[1], half, half, [(st.at[1], half), (rd.at[1], 0)])
    xb = push(bottom(st.at[1]), bottom(rx), sx, 9)
    cs[3].wait_recv()
    product(7, so, rs.at[3])
    xt.wait_recv()
    yt.wait_recv()
    add(out_ref, 0, half, [(so, 0), (rx, 0), (ry, 0)])
    yb.wait_recv()
    xb.wait_recv()
    add(out_ref, half, half, [(so, half), (rx, half), (ry, half)])
    for c in (*cs, dt, db, xt, yb, yt, xb):
        c.wait_send()


def down_scattered(x, w_down, cid):
    rows, hidden = x.shape
    n = lax.axis_size("seq")
    width = w_down.shape[2] // n
    b = x.dtype
    return pl.pallas_call(
        functools.partial(_down_kernel, rows, width, 256),
        out_shape=jax.ShapeDtypeStruct((rows, width), b),
        in_specs=[pl.BlockSpec(memory_space=VMEM), pl.BlockSpec(memory_space=pl.ANY)],
        out_specs=pl.BlockSpec(memory_space=VMEM),
        scratch_shapes=[
            VMEM((n, hidden, width), b),
            VMEM((4, rows, width), b),
            VMEM((4, rows, width), b),
            VMEM((3, rows, width), b),
            VMEM((rows, width), jnp.float32),
            VMEM((2, rows // 2, width), b),
            VMEM((rows, width), b),
            VMEM((rows, width), b),
            pltpu.SemaphoreType.DMA((n,)),
            pltpu.SemaphoreType.DMA((10,)),
            pltpu.SemaphoreType.DMA((10,)),
        ],
        compiler_params=pltpu.CompilerParams(
            collective_id=cid, has_side_effects=True, vmem_limit_bytes=52 << 20
        ),
    )(x, w_down)


def by_heads(
    query_proj,
    key_proj,
    value_proj,
    residual,
    out_weight,
    expert_ids,
    gate_values,
    w_gate,
    w_up,
    w_down,
):
    n_seq, groups = lax.axis_size("seq"), lax.axis_size("exp")
    block = query_proj.shape[0]
    tokens = n_seq * block
    tok_sub = residual.shape[0]
    width = residual.shape[1] // n_seq
    plane = n_seq * tok_sub
    capacity = max(2, (3 * tok_sub * TOP + 2 * groups - 1) // (2 * groups))
    bf, f32 = jnp.bfloat16, jnp.float32
    meta = jnp.concatenate(
        [expert_ids.T.astype(f32), gate_values.T, jnp.zeros((8 - 2 * TOP, tok_sub), f32)], axis=0
    )
    meta = jnp.pad(meta, ((0, 0), (0, 128 - tok_sub)))
    head = ("col", HD, "row", block)
    q, k, v, res, meta = exchange(
        "seq",
        (head, head, head, ("col", width, "row", tok_sub), ("all", 0, "row", 8)),
        (query_proj, key_proj, value_proj, residual, meta),
        [jax.ShapeDtypeStruct((tokens, HD), bf)] * 3
        + [jax.ShapeDtypeStruct((plane, width), bf), jax.ShapeDtypeStruct((8 * n_seq, 128), f32)],
        0,
    )
    qf = features(q).reshape(n_seq, block, HD)
    kf = features(k).reshape(n_seq, block, HD)
    vr = v.reshape(n_seq, block, HD)
    states = jnp.einsum("btd,bte->bde", kf, vr, preferred_element_type=f32)
    running, before_it = jnp.zeros_like(states[0]), []
    for b in range(n_seq):
        before_it.append(running)
        running = running + states[b]
    prefix = jnp.stack(before_it).astype(bf)
    scores = jnp.einsum("btd,bsd->bts", qf, kf, preferred_element_type=f32)
    causal = jnp.arange(block)[:, None] >= jnp.arange(block)[None, :]
    weights = jnp.where(causal[None], scores, 0.0).astype(bf)
    combined = jnp.einsum("bts,bse->bte", weights, vr, preferred_element_type=f32)
    combined = combined + jnp.einsum("btd,bde->bte", qf, prefix, preferred_element_type=f32)
    normed = combined * lax.rsqrt(jnp.mean(combined * combined, axis=-1, keepdims=True) + 1e-06)
    normed = normed.astype(bf).reshape(n_seq, groups, tok_sub, HD)
    normed = normed.transpose(1, 0, 2, 3).reshape(tokens, HD)

    partial_out = times_rows(gather_columns(normed, 1), out_weight).astype(bf)
    (parts,) = exchange(
        "exp",
        (("row", plane, "row", plane),),
        (partial_out,),
        [jax.ShapeDtypeStruct((tokens, width), bf)],
        2,
    )
    summed = jnp.sum(parts.reshape(groups, plane, width).astype(f32), axis=0)
    mixed_in = (res.astype(f32) + summed).astype(bf)

    meta = meta.reshape(n_seq, 8, 128)
    ids = meta[:, :TOP, :tok_sub].astype(jnp.int32).transpose(0, 2, 1)
    gates = meta[:, TOP : 2 * TOP, :tok_sub].transpose(0, 2, 1).reshape(plane, TOP)
    chosen = ids.reshape(n_seq, tok_sub * TOP)
    onehot = (chosen[:, :, None] == jnp.arange(groups, dtype=jnp.int32)).astype(jnp.int32)
    earlier = (jnp.arange(tok_sub * TOP)[:, None] > jnp.arange(tok_sub * TOP)[None, :])
    before = jnp.sum(earlier[None, :, :, None] * onehot[:, None, :, :], axis=2)
    slot = jnp.sum(before * onehot, axis=2)
    target = (chosen * n_seq + jnp.arange(n_seq, dtype=jnp.int32)[:, None]) * capacity + slot
    target = target.reshape(plane, TOP)
    slots = jnp.arange(groups * n_seq * capacity, dtype=jnp.int32)
    picks = [(target[:, j : j + 1] == slots[None, :]).astype(bf) for j in range(TOP)]
    placing = picks[0]
    for p in picks[1:]:
        placing = placing + p
    outgoing = lax.dot_general(
        placing, mixed_in, (((0,), (0,)), ((), ())), preferred_element_type=f32
    ).astype(bf)
    load = n_seq * capacity
    rows_shape = [jax.ShapeDtypeStruct((groups * load, width), bf)]
    (arrived,) = exchange("exp", (("row", load, "row", load),), (outgoing,), rows_shape, 3)
    activated = gathered_up(arrived, w_gate, w_up, 4)
    sums = down_scattered(activated, w_down, 5)
    (returned,) = exchange("exp", (("row", load, "row", load),), (sums,), rows_shape, 6)
    mixed = mixed_in.astype(f32)
    extra = jnp.zeros_like(mixed)
    for j in range(TOP):
        picked = jnp.dot(picks[j], returned, preferred_element_type=f32)
        extra = extra + gates[:, j : j + 1] * picked
    mixed = (mixed + extra).astype(bf)
    (out,) = exchange(
        "seq",
        (("row", tok_sub, "col", width),),
        (mixed,),
        [jax.ShapeDtypeStruct(residual.shape, bf)],
        7,
    )
    return out


def solution(mesh):
    return jax.shard_map(
        by_heads if mesh.shape["seq"] == 8 and mesh.shape["exp"] == 4 else local,
        mesh=mesh,
        in_specs=(
            P("seq", "exp"),
            P("seq", "exp"),
            P("seq", "exp"),
            P(("seq", "exp"), None),
            P("seq", "exp"),
            P(("seq", "exp"), None),
            P(("seq", "exp"), None),
            P("exp", "seq", None),
            P("exp", "seq", None),
            P("exp", "seq", None),
        ),
        out_specs=P(("seq", "exp"), None),
        check_vma=False,
    )
```

```python
import functools

import jax
import jax.numpy as jnp
from jax import lax
from jax.experimental import pallas as pl
from jax.experimental.pallas import tpu as pltpu
from jax.sharding import PartitionSpec as P

HD = 128
TOP = 2


def entering(array, axis, combine, identity):
    devices, place = (lax.axis_size(axis), lax.axis_index(axis))
    everything = lax.all_gather(array.astype(jnp.bfloat16), axis)
    start = jnp.broadcast_to(jnp.asarray(identity, array.dtype), array.shape)

    def hop(k, before):
        reached = k < place
        new = combine(before, everything[k].astype(array.dtype))
        return jnp.where(reached, new, before)

    return lax.fori_loop(0, devices, hop, start)


def features(x):
    widened = x.astype(jnp.float32)
    return (widened * jax.nn.sigmoid(widened)).astype(jnp.bfloat16)


def times_rows(left, right):
    return lax.dot_general(
        left, right, (((1,), (1,)), ((), ())), preferred_element_type=jnp.float32
    )


def local(
    query_proj,
    key_proj,
    value_proj,
    residual,
    out_weight,
    expert_ids,
    gate_values,
    w_gate,
    w_up,
    w_down,
):
    tokens_here = query_proj.shape[0]
    heads_here = query_proj.shape[1] // HD
    query_feat = features(query_proj).reshape(tokens_here, heads_here, HD)
    key_feat = features(key_proj).reshape(tokens_here, heads_here, HD)
    value_rows = value_proj.reshape(tokens_here, heads_here, HD)
    span_state = jnp.einsum(
        "thd,the->hde", key_feat, value_rows, preferred_element_type=jnp.float32
    )
    earlier = entering(span_state, "seq", lambda a, b: a + b, jnp.zeros_like(span_state))
    prefix = earlier.astype(jnp.bfloat16)
    earlier_term = jnp.einsum(
        "thd,hde->the", query_feat, prefix, preferred_element_type=jnp.float32
    )
    scores = jnp.einsum("thd,shd->hts", query_feat, key_feat, preferred_element_type=jnp.float32)
    causal = jnp.arange(tokens_here)[:, None] >= jnp.arange(tokens_here)[None, :]
    weights = jnp.where(causal[None], scores, 0.0).astype(jnp.bfloat16)
    local_term = jnp.einsum("hts,she->the", weights, value_rows, preferred_element_type=jnp.float32)
    combined = local_term + earlier_term
    normed = combined * lax.rsqrt(jnp.mean(combined * combined, axis=-1, keepdims=True) + 1e-06)
    normed = normed.astype(jnp.bfloat16).reshape(tokens_here, heads_here * HD)
    partial_out = times_rows(normed, lax.all_gather(out_weight, "seq", axis=0, tiled=True))
    summed = lax.psum_scatter(
        partial_out.astype(jnp.bfloat16), "exp", scatter_dimension=0, tiled=True
    ).astype(jnp.float32)
    mixed_in = (residual.astype(jnp.float32) + summed).astype(jnp.bfloat16)
    groups = lax.axis_size("exp")
    tok_sub = residual.shape[0]
    capacity = max(2, (3 * tok_sub * TOP + 2 * groups - 1) // (2 * groups))
    local_rows = groups * capacity
    chosen = expert_ids.reshape(-1)
    onehot = (chosen[:, None] == jnp.arange(groups, dtype=jnp.int32)[None, :]).astype(jnp.int32)
    place = jnp.arange(tok_sub * TOP)
    before = jnp.sum((place[:, None] > place[None, :])[:, :, None] * onehot[None], axis=1)
    slot_index = jnp.sum(before * onehot, axis=1)
    target = chosen * capacity + slot_index
    targets = target.reshape(tok_sub, TOP)
    slot_ids = jnp.arange(local_rows, dtype=jnp.int32)
    placing = jnp.any(slot_ids[:, None, None] == targets[None, :, :], axis=2).astype(jnp.bfloat16)
    outgoing = jnp.dot(placing, mixed_in, preferred_element_type=jnp.float32).astype(jnp.bfloat16)
    outgoing = outgoing.reshape(groups, capacity, -1)
    gate_local = w_gate[0]
    up_local = w_up[0]
    down_local = w_down[0]
    hidden_here = gate_local.shape[0]
    arrived = lax.all_to_all(outgoing, "exp", split_axis=0, concat_axis=0, tiled=True).reshape(
        local_rows, -1
    )
    rows_part = lax.all_gather(arrived, "seq", axis=0, tiled=True)
    acts = jnp.concatenate(
        [times_rows(rows_part, gate_local), times_rows(rows_part, up_local)], axis=1
    )
    gate_act = acts[:, :hidden_here]
    up_act = acts[:, hidden_here:]
    activated = (jax.nn.silu(gate_act) * up_act).astype(jnp.bfloat16)
    rows_part = activated
    expert_sums = lax.psum_scatter(
        jnp.dot(rows_part, down_local, preferred_element_type=jnp.float32).astype(jnp.bfloat16),
        "seq",
        scatter_dimension=0,
        tiled=True,
    )
    expert_out = expert_sums.reshape(groups, capacity, -1)
    returned = lax.all_to_all(expert_out, "exp", split_axis=0, concat_axis=0, tiled=True).reshape(
        local_rows, -1
    )
    picked = returned[target].astype(jnp.float32).reshape(tok_sub, TOP, -1)
    mixed = mixed_in.astype(jnp.float32) + jnp.sum(gate_values[:, :, None] * picked, axis=1)
    return mixed.astype(jnp.bfloat16)


MESH = pl.DeviceIdType.MESH
VMEM = pltpu.VMEM


def _place(ref, kind, size, i):
    if kind == "row":
        return ref.at[pl.ds(pl.multiple_of(i * size, size), size), :]
    if kind == "col":
        return ref.at[:, pl.ds(pl.multiple_of(i * size, size), size)]
    return ref


def _here(axis, peers):
    barrier = pltpu.get_barrier_semaphore()
    for peer in peers:
        pl.semaphore_signal(barrier, inc=1, device_id={axis: peer}, device_id_type=MESH)


def _greet(axis, peers):
    _here(axis, peers)
    pl.semaphore_wait(pltpu.get_barrier_semaphore(), len(peers))


def _exchange_kernel(axis, n, kinds, *refs):
    m = len(kinds)
    ins, outs = refs[:m], refs[m : 2 * m]
    send, recv, own = refs[2 * m :]
    me = lax.axis_index(axis)
    peers = [lax.rem(me + k, n) for k in range(1, n)]
    _greet(axis, peers)
    copies = []
    for k, peer in enumerate(peers):
        for a, (sk, ss, dk, ds) in enumerate(kinds):
            c = pltpu.make_async_remote_copy(
                src_ref=_place(ins[a], sk, ss, peer),
                dst_ref=_place(outs[a], dk, ds, me),
                send_sem=send.at[a, k],
                recv_sem=recv.at[a, k],
                device_id={axis: peer},
                device_id_type=MESH,
            )
            c.start()
            copies.append(c)
    for a, (sk, ss, dk, ds) in enumerate(kinds):
        c = pltpu.make_async_copy(
            _place(ins[a], sk, ss, me), _place(outs[a], dk, ds, me), own.at[a]
        )
        c.start()
        copies.append(c)
    for c in copies:
        c.wait()


def exchange(axis, kinds, ins, out_shapes, cid, source=VMEM):
    n, m = lax.axis_size(axis), len(ins)
    return pl.pallas_call(
        functools.partial(_exchange_kernel, axis, n, kinds),
        out_shape=out_shapes,
        in_specs=[pl.BlockSpec(memory_space=source)] * m,
        out_specs=[pl.BlockSpec(memory_space=VMEM)] * m,
        scratch_shapes=[
            pltpu.SemaphoreType.DMA((m, n - 1)),
            pltpu.SemaphoreType.DMA((m, n - 1)),
            pltpu.SemaphoreType.DMA((m,)),
        ],
        compiler_params=pltpu.CompilerParams(
            collective_id=cid, has_side_effects=True, vmem_limit_bytes=(32 if source is VMEM else 62) << 20
        ),
    )(*ins)


def _around(s):
    c, x, y = lax.rem(s, 2), lax.rem(s // 2, 2), s // 4
    right = s + 2 - 4 * x
    up = s + 4 - 8 * y
    return right, up, up + 2 - 4 * x, 1 - 2 * c


def _gather_kernel(rows, width, in_ref, out_ref, send, recv, own):
    s = lax.axis_index("seq")
    sx, sy, sd, flip = _around(s)
    sib = s + flip
    half = rows // 2

    def at(i, part=None):
        cols = pl.ds(pl.multiple_of(i * width, width), width)
        if part is None:
            return out_ref.at[:, cols]
        return out_ref.at[pl.ds(part * half, half), cols]

    def push(src, dst, to, k):
        c = pltpu.make_async_remote_copy(
            src_ref=src, dst_ref=dst, send_sem=send.at[k], recv_sem=recv.at[k],
            device_id={"seq": to}, device_id_type=MESH,
        )
        c.start()
        return c

    _greet("seq", [sx, sy, sib])
    to_x = push(in_ref, at(s), sx, 0)
    to_y = push(in_ref, at(s), sy, 1)
    to_s = push(in_ref, at(s), sib, 2)
    mine = pltpu.make_async_copy(in_ref, at(s), own)
    mine.start()
    to_x.wait_recv()
    fy = push(at(sx, 0), at(sx, 0), sy, 3)
    gx = push(at(sx), at(sx), sib, 4)
    to_y.wait_recv()
    fx = push(at(sy, 1), at(sy, 1), sx, 5)
    gy = push(at(sy), at(sy), sib, 6)
    fy.wait_recv()
    fx.wait_recv()
    gd = push(at(sd), at(sd), sib, 7)
    to_s.wait_recv()
    gx.wait_recv()
    gy.wait_recv()
    gd.wait_recv()
    for c in (to_x, to_y, to_s, fy, gx, fx, gy, gd):
        c.wait_send()
    mine.wait()


def gather_columns(x, cid):
    rows, width = x.shape
    n = lax.axis_size("seq")
    return pl.pallas_call(
        functools.partial(_gather_kernel, rows, width),
        out_shape=jax.ShapeDtypeStruct((rows, n * width), x.dtype),
        in_specs=[pl.BlockSpec(memory_space=VMEM)],
        out_specs=pl.BlockSpec(memory_space=VMEM),
        scratch_shapes=[
            pltpu.SemaphoreType.DMA((8,)),
            pltpu.SemaphoreType.DMA((8,)),
            pltpu.SemaphoreType.DMA,
        ],
        compiler_params=pltpu.CompilerParams(
            collective_id=cid, has_side_effects=True, vmem_limit_bytes=32 << 20
        ),
    )(x)


def _pusher(send, recv):
    def push(src, dst, to, k):
        c = pltpu.make_async_remote_copy(
            src_ref=src, dst_ref=dst, send_sem=send.at[k], recv_sem=recv.at[k],
            device_id={"seq": to}, device_id_type=MESH,
        )
        c.start()
        return c

    return push


def _up_kernel(
    rows, width, tile, in_ref, gate_hbm, up_hbm, out_ref, all_rows, acc, held, wsem, send, recv, own
):
    s = lax.axis_index("seq")
    sx, sy, sd, flip = _around(s)
    sib = s + flip
    half = rows // 2
    pair = 2 * width
    hidden = out_ref.shape[1]
    chips = [i // 2 for i in (s, sx, sy, sd)]
    _here("seq", [sx, sy, sib])
    loads = []
    for k, chip in enumerate(chips):
        for m, hbm in enumerate((gate_hbm, up_hbm)):
            c = pltpu.make_async_copy(
                hbm.at[0, :, pl.ds(pl.multiple_of(chip * pair, pair), pair)],
                held.at[k, m],
                wsem.at[k, m],
            )
            c.start()
            loads.append(c)
    push = _pusher(send, recv)

    def at(i, part=None):
        cols = pl.ds(pl.multiple_of(i * width, width), width)
        if part is None:
            return all_rows.at[:, cols]
        return all_rows.at[pl.ds(part * half, half), cols]

    def multiply(k):
        loads[2 * k].wait()
        loads[2 * k + 1].wait()
        left = pl.ds(pl.multiple_of(chips[k] * pair, pair), pair)

        @pl.loop(0, hidden // tile)
        def _(j):
            at_j = pl.ds(pl.multiple_of(j * tile, tile), tile)
            x = all_rows[:, left]
            g = times_rows(x, held[k, 0, at_j, :])
            u = times_rows(x, held[k, 1, at_j, :])
            if k:
                g = g + acc[0, :, at_j]
                u = u + acc[1, :, at_j]
            if k < 3:
                acc[0, :, at_j] = g
                acc[1, :, at_j] = u
            else:
                out_ref[:, at_j] = (g / (1.0 + jnp.exp(-g)) * u).astype(out_ref.dtype)

    pl.semaphore_wait(pltpu.get_barrier_semaphore(), 3)
    to_x = push(in_ref, at(s), sx, 0)
    to_y = push(in_ref, at(s), sy, 1)
    to_s = push(in_ref, at(s), sib, 2)
    mine = pltpu.make_async_copy(in_ref, at(s), own)
    mine.start()
    mine.wait()
    to_s.wait_recv()
    multiply(0)
    to_x.wait_recv()
    fy = push(at(sx, 0), at(sx, 0), sy, 3)
    gx = push(at(sx), at(sx), sib, 4)
    to_y.wait_recv()
    fx = push(at(sy, 1), at(sy, 1), sx, 5)
    gy = push(at(sy), at(sy), sib, 6)
    gx.wait_recv()
    multiply(1)
    gy.wait_recv()
    multiply(2)
    fy.wait_recv()
    fx.wait_recv()
    gd = push(at(sd), at(sd), sib, 7)
    gd.wait_recv()
    multiply(3)
    for c in (to_x, to_y, to_s, fy, gx, fx, gy, gd):
        c.wait_send()


def gathered_up(x, w_gate, w_up, cid):
    rows, width = x.shape
    hidden = w_gate.shape[1]
    n = lax.axis_size("seq")
    return pl.pallas_call(
        functools.partial(_up_kernel, rows, width, 384),
        out_shape=jax.ShapeDtypeStruct((rows, hidden), x.dtype),
        in_specs=[pl.BlockSpec(memory_space=VMEM)] + [pl.BlockSpec(memory_space=pl.ANY)] * 2,
        out_specs=pl.BlockSpec(memory_space=VMEM),
        scratch_shapes=[
            VMEM((rows, n * width), x.dtype),
            VMEM((2, rows, hidden), jnp.float32),
            VMEM((4, 2, hidden, 2 * width), x.dtype),
            pltpu.SemaphoreType.DMA((4, 2)),
            pltpu.SemaphoreType.DMA((8,)),
            pltpu.SemaphoreType.DMA((8,)),
            pltpu.SemaphoreType.DMA,
        ],
        compiler_params=pltpu.CompilerParams(
            collective_id=cid, has_side_effects=True, vmem_limit_bytes=52 << 20
        ),
    )(x, w_gate, w_up)


def _down_kernel(
    rows, width, tile, in_ref, down_hbm, out_ref, held, sb, rs, st, so, rd, rx, ry, wsem, send, recv
):
    s = lax.axis_index("seq")
    sx, sy, sd, flip = _around(s)
    sib = s + flip
    half = rows // 2
    step = 32
    order = [sd + flip, sx + flip, sd, sy + flip, sx, sy, s + flip, s]
    _here("seq", [sx, sy, sib])
    loads = []
    for k, i in enumerate(order):
        c = pltpu.make_async_copy(
            down_hbm.at[0, :, pl.ds(pl.multiple_of(i * width, width), width)],
            held.at[k],
            wsem.at[k],
        )
        c.start()
        loads.append(c)
    push = _pusher(send, recv)

    def product(k, dst, more=None):
        loads[k].wait()

        @pl.loop(0, width // tile)
        def _(j):
            at_j = pl.ds(pl.multiple_of(j * tile, tile), tile)
            r = jnp.dot(in_ref[...], held[k, :, at_j], preferred_element_type=jnp.float32)
            if more is not None:
                r = r + more[:, at_j].astype(jnp.float32)
            dst[:, at_j] = r.astype(dst.dtype)

    def add(dst, d0, count, terms):
        @pl.loop(0, count // step)
        def _(i):
            total = None
            for ref, base in terms:
                v = ref[pl.ds(pl.multiple_of(base + i * step, step), step), :].astype(jnp.float32)
                total = v if total is None else total + v
            dst[pl.ds(pl.multiple_of(d0 + i * step, step), step), :] = total.astype(dst.dtype)

    def top(ref):
        return ref.at[pl.ds(0, half), :]

    def bottom(ref):
        return ref.at[pl.ds(half, half), :]

    product(0, sb.at[0])
    pl.semaphore_wait(pltpu.get_barrier_semaphore(), 3)
    cs = [push(sb.at[0], rs.at[0], sib, 0)]
    product(1, sb.at[1])
    cs.append(push(sb.at[1], rs.at[1], sib, 1))
    cs[0].wait_recv()
    product(2, st.at[0], rs.at[0])
    dt = push(top(st.at[0]), rd.at[0], sx, 4)
    db = push(bottom(st.at[0]), rd.at[1], sy, 5)
    product(3, sb.at[2])
    cs.append(push(sb.at[2], rs.at[2], sib, 2))
    cs[1].wait_recv()
    product(4, st.at[1], rs.at[1])
    xt = push(top(st.at[1]), top(rx), sx, 6)
    cs[2].wait_recv()
    product(5, st.at[2], rs.at[2])
    yb = push(bottom(st.at[2]), bottom(ry), sy, 7)
    product(6, sb.at[3])
    cs.append(push(sb.at[3], rs.at[3], sib, 3))
    dt.wait_recv()
    add(st.at[2], 0, half, [(st.at[2], 0), (rd.at[0], 0)])
    yt = push(top(st.at[2]), top(ry), sy, 8)
    db.wait_recv()
    add(st.at[1], half, half, [(st.at[1], half), (rd.at[1], 0)])
    xb = push(bottom(st.at[1]), bottom(rx), sx, 9)
    cs[3].wait_recv()
    product(7, so, rs.at[3])
    xt.wait_recv()
    yt.wait_recv()
    add(out_ref, 0, half, [(so, 0), (rx, 0), (ry, 0)])
    yb.wait_recv()
    xb.wait_recv()
    add(out_ref, half, half, [(so, half), (rx, half), (ry, half)])
    for c in (*cs, dt, db, xt, yb, yt, xb):
        c.wait_send()


def down_scattered(x, w_down, cid):
    rows, hidden = x.shape
    n = lax.axis_size("seq")
    width = w_down.shape[2] // n
    b = x.dtype
    return pl.pallas_call(
        functools.partial(_down_kernel, rows, width, 256),
        out_shape=jax.ShapeDtypeStruct((rows, width), b),
        in_specs=[pl.BlockSpec(memory_space=VMEM), pl.BlockSpec(memory_space=pl.ANY)],
        out_specs=pl.BlockSpec(memory_space=VMEM),
        scratch_shapes=[
            VMEM((n, hidden, width), b),
            VMEM((4, rows, width), b),
            VMEM((4, rows, width), b),
            VMEM((3, rows, width), b),
            VMEM((rows, width), jnp.float32),
            VMEM((2, rows // 2, width), b),
            VMEM((rows, width), b),
            VMEM((rows, width), b),
            pltpu.SemaphoreType.DMA((n,)),
            pltpu.SemaphoreType.DMA((10,)),
            pltpu.SemaphoreType.DMA((10,)),
        ],
        compiler_params=pltpu.CompilerParams(
            collective_id=cid, has_side_effects=True, vmem_limit_bytes=52 << 20
        ),
    )(x, w_down)


def by_heads(
    query_proj,
    key_proj,
    value_proj,
    residual,
    out_weight,
    expert_ids,
    gate_values,
    w_gate,
    w_up,
    w_down,
):
    n_seq, groups = lax.axis_size("seq"), lax.axis_size("exp")
    block = query_proj.shape[0]
    tokens = n_seq * block
    tok_sub = residual.shape[0]
    width = residual.shape[1] // n_seq
    plane = n_seq * tok_sub
    capacity = max(2, (3 * tok_sub * TOP + 2 * groups - 1) // (2 * groups))
    bf, f32 = jnp.bfloat16, jnp.float32
    meta = jnp.concatenate(
        [expert_ids.T.astype(f32), gate_values.T, jnp.zeros((8 - 2 * TOP, tok_sub), f32)], axis=0
    )
    meta = jnp.pad(meta, ((0, 0), (0, 128 - tok_sub)))
    head = ("col", HD, "row", block)
    q, k, v, res, meta = exchange(
        "seq",
        (head, head, head, ("col", width, "row", tok_sub), ("all", 0, "row", 8)),
        (query_proj, key_proj, value_proj, residual, meta),
        [jax.ShapeDtypeStruct((tokens, HD), bf)] * 3
        + [jax.ShapeDtypeStruct((plane, width), bf), jax.ShapeDtypeStruct((8 * n_seq, 128), f32)],
        0,
        pl.ANY,
    )
    qf = features(q).reshape(n_seq, block, HD)
    kf = features(k).reshape(n_seq, block, HD)
    vr = v.reshape(n_seq, block, HD)
    states = jnp.einsum("btd,bte->bde", kf, vr, preferred_element_type=f32)
    running, before_it = jnp.zeros_like(states[0]), []
    for b in range(n_seq):
        before_it.append(running)
        running = running + states[b]
    prefix = jnp.stack(before_it).astype(bf)
    scores = jnp.einsum("btd,bsd->bts", qf, kf, preferred_element_type=f32)
    causal = jnp.arange(block)[:, None] >= jnp.arange(block)[None, :]
    weights = jnp.where(causal[None], scores, 0.0).astype(bf)
    combined = jnp.einsum("bts,bse->bte", weights, vr, preferred_element_type=f32)
    combined = combined + jnp.einsum("btd,bde->bte", qf, prefix, preferred_element_type=f32)
    normed = combined * lax.rsqrt(jnp.mean(combined * combined, axis=-1, keepdims=True) + 1e-06)
    normed = normed.astype(bf).reshape(n_seq, groups, tok_sub, HD)
    normed = normed.transpose(1, 0, 2, 3).reshape(tokens, HD)

    partial_out = times_rows(gather_columns(normed, 1), out_weight).astype(bf)
    (parts,) = exchange(
        "exp",
        (("row", plane, "row", plane),),
        (partial_out,),
        [jax.ShapeDtypeStruct((tokens, width), bf)],
        2,
    )
    summed = jnp.sum(parts.reshape(groups, plane, width).astype(f32), axis=0)
    mixed_in = (res.astype(f32) + summed).astype(bf)

    meta = meta.reshape(n_seq, 8, 128)
    ids = meta[:, :TOP, :tok_sub].astype(jnp.int32).transpose(0, 2, 1)
    gates = meta[:, TOP : 2 * TOP, :tok_sub].transpose(0, 2, 1).reshape(plane, TOP)
    chosen = ids.reshape(n_seq, tok_sub * TOP)
    onehot = (chosen[:, :, None] == jnp.arange(groups, dtype=jnp.int32)).astype(jnp.int32)
    earlier = (jnp.arange(tok_sub * TOP)[:, None] > jnp.arange(tok_sub * TOP)[None, :])
    before = jnp.sum(earlier[None, :, :, None] * onehot[:, None, :, :], axis=2)
    slot = jnp.sum(before * onehot, axis=2)
    target = (chosen * n_seq + jnp.arange(n_seq, dtype=jnp.int32)[:, None]) * capacity + slot
    target = target.reshape(plane, TOP)
    slots = jnp.arange(groups * n_seq * capacity, dtype=jnp.int32)
    picks = [(target[:, j : j + 1] == slots[None, :]).astype(bf) for j in range(TOP)]
    placing = picks[0]
    for p in picks[1:]:
        placing = placing + p
    outgoing = lax.dot_general(
        placing, mixed_in, (((0,), (0,)), ((), ())), preferred_element_type=f32
    ).astype(bf)
    load = n_seq * capacity
    rows_shape = [jax.ShapeDtypeStruct((groups * load, width), bf)]
    (arrived,) = exchange("exp", (("row", load, "row", load),), (outgoing,), rows_shape, 3)
    activated = gathered_up(arrived, w_gate, w_up, 4)
    sums = down_scattered(activated, w_down, 5)
    (returned,) = exchange("exp", (("row", load, "row", load),), (sums,), rows_shape, 6)
    mixed = mixed_in.astype(f32)
    extra = jnp.zeros_like(mixed)
    for j in range(TOP):
        picked = jnp.dot(picks[j], returned, preferred_element_type=f32)
        extra = extra + gates[:, j : j + 1] * picked
    mixed = (mixed + extra).astype(bf)
    (out,) = exchange(
        "seq",
        (("row", tok_sub, "col", width),),
        (mixed,),
        [jax.ShapeDtypeStruct(residual.shape, bf)],
        7,
    )
    return out


def solution(mesh):
    return jax.shard_map(
        by_heads if mesh.shape["seq"] == 8 and mesh.shape["exp"] == 4 else local,
        mesh=mesh,
        in_specs=(
            P("seq", "exp"),
            P("seq", "exp"),
            P("seq", "exp"),
            P(("seq", "exp"), None),
            P("seq", "exp"),
            P(("seq", "exp"), None),
            P(("seq", "exp"), None),
            P("exp", "seq", None),
            P("exp", "seq", None),
            P("exp", "seq", None),
        ),
        out_specs=P(("seq", "exp"), None),
        check_vma=False,
    )
```

```python
import functools

import jax
import jax.numpy as jnp
from jax import lax
from jax.experimental import pallas as pl
from jax.experimental.pallas import tpu as pltpu
from jax.sharding import PartitionSpec as P

HD = 128
TOP = 2


def entering(array, axis, combine, identity):
    devices, place = (lax.axis_size(axis), lax.axis_index(axis))
    everything = lax.all_gather(array.astype(jnp.bfloat16), axis)
    start = jnp.broadcast_to(jnp.asarray(identity, array.dtype), array.shape)

    def hop(k, before):
        reached = k < place
        new = combine(before, everything[k].astype(array.dtype))
        return jnp.where(reached, new, before)

    return lax.fori_loop(0, devices, hop, start)


def features(x):
    widened = x.astype(jnp.float32)
    return (widened * jax.nn.sigmoid(widened)).astype(jnp.bfloat16)


def times_rows(left, right):
    return lax.dot_general(
        left, right, (((1,), (1,)), ((), ())), preferred_element_type=jnp.float32
    )


def local(
    query_proj,
    key_proj,
    value_proj,
    residual,
    out_weight,
    expert_ids,
    gate_values,
    w_gate,
    w_up,
    w_down,
):
    tokens_here = query_proj.shape[0]
    heads_here = query_proj.shape[1] // HD
    query_feat = features(query_proj).reshape(tokens_here, heads_here, HD)
    key_feat = features(key_proj).reshape(tokens_here, heads_here, HD)
    value_rows = value_proj.reshape(tokens_here, heads_here, HD)
    span_state = jnp.einsum(
        "thd,the->hde", key_feat, value_rows, preferred_element_type=jnp.float32
    )
    earlier = entering(span_state, "seq", lambda a, b: a + b, jnp.zeros_like(span_state))
    prefix = earlier.astype(jnp.bfloat16)
    earlier_term = jnp.einsum(
        "thd,hde->the", query_feat, prefix, preferred_element_type=jnp.float32
    )
    scores = jnp.einsum("thd,shd->hts", query_feat, key_feat, preferred_element_type=jnp.float32)
    causal = jnp.arange(tokens_here)[:, None] >= jnp.arange(tokens_here)[None, :]
    weights = jnp.where(causal[None], scores, 0.0).astype(jnp.bfloat16)
    local_term = jnp.einsum("hts,she->the", weights, value_rows, preferred_element_type=jnp.float32)
    combined = local_term + earlier_term
    normed = combined * lax.rsqrt(jnp.mean(combined * combined, axis=-1, keepdims=True) + 1e-06)
    normed = normed.astype(jnp.bfloat16).reshape(tokens_here, heads_here * HD)
    partial_out = times_rows(normed, lax.all_gather(out_weight, "seq", axis=0, tiled=True))
    summed = lax.psum_scatter(
        partial_out.astype(jnp.bfloat16), "exp", scatter_dimension=0, tiled=True
    ).astype(jnp.float32)
    mixed_in = (residual.astype(jnp.float32) + summed).astype(jnp.bfloat16)
    groups = lax.axis_size("exp")
    tok_sub = residual.shape[0]
    capacity = max(2, (3 * tok_sub * TOP + 2 * groups - 1) // (2 * groups))
    local_rows = groups * capacity
    chosen = expert_ids.reshape(-1)
    onehot = (chosen[:, None] == jnp.arange(groups, dtype=jnp.int32)[None, :]).astype(jnp.int32)
    place = jnp.arange(tok_sub * TOP)
    before = jnp.sum((place[:, None] > place[None, :])[:, :, None] * onehot[None], axis=1)
    slot_index = jnp.sum(before * onehot, axis=1)
    target = chosen * capacity + slot_index
    targets = target.reshape(tok_sub, TOP)
    slot_ids = jnp.arange(local_rows, dtype=jnp.int32)
    placing = jnp.any(slot_ids[:, None, None] == targets[None, :, :], axis=2).astype(jnp.bfloat16)
    outgoing = jnp.dot(placing, mixed_in, preferred_element_type=jnp.float32).astype(jnp.bfloat16)
    outgoing = outgoing.reshape(groups, capacity, -1)
    gate_local = w_gate[0]
    up_local = w_up[0]
    down_local = w_down[0]
    hidden_here = gate_local.shape[0]
    arrived = lax.all_to_all(outgoing, "exp", split_axis=0, concat_axis=0, tiled=True).reshape(
        local_rows, -1
    )
    rows_part = lax.all_gather(arrived, "seq", axis=0, tiled=True)
    acts = jnp.concatenate(
        [times_rows(rows_part, gate_local), times_rows(rows_part, up_local)], axis=1
    )
    gate_act = acts[:, :hidden_here]
    up_act = acts[:, hidden_here:]
    activated = (jax.nn.silu(gate_act) * up_act).astype(jnp.bfloat16)
    rows_part = activated
    expert_sums = lax.psum_scatter(
        jnp.dot(rows_part, down_local, preferred_element_type=jnp.float32).astype(jnp.bfloat16),
        "seq",
        scatter_dimension=0,
        tiled=True,
    )
    expert_out = expert_sums.reshape(groups, capacity, -1)
    returned = lax.all_to_all(expert_out, "exp", split_axis=0, concat_axis=0, tiled=True).reshape(
        local_rows, -1
    )
    picked = returned[target].astype(jnp.float32).reshape(tok_sub, TOP, -1)
    mixed = mixed_in.astype(jnp.float32) + jnp.sum(gate_values[:, :, None] * picked, axis=1)
    return mixed.astype(jnp.bfloat16)


MESH = pl.DeviceIdType.MESH
VMEM = pltpu.VMEM


def _place(ref, kind, size, i):
    if kind == "row":
        return ref.at[pl.ds(pl.multiple_of(i * size, size), size), :]
    if kind == "col":
        return ref.at[:, pl.ds(pl.multiple_of(i * size, size), size)]
    return ref


def _here(axis, peers):
    barrier = pltpu.get_barrier_semaphore()
    for peer in peers:
        pl.semaphore_signal(barrier, inc=1, device_id={axis: peer}, device_id_type=MESH)


def _greet(axis, peers):
    _here(axis, peers)
    pl.semaphore_wait(pltpu.get_barrier_semaphore(), len(peers))


def _exchange_kernel(axis, n, kinds, *refs):
    m = len(kinds)
    ins, outs = refs[:m], refs[m : 2 * m]
    send, recv, own = refs[2 * m :]
    me = lax.axis_index(axis)
    peers = [lax.rem(me + k, n) for k in range(1, n)]
    _greet(axis, peers)
    copies = []
    for k, peer in enumerate(peers):
        for a, (sk, ss, dk, ds) in enumerate(kinds):
            c = pltpu.make_async_remote_copy(
                src_ref=_place(ins[a], sk, ss, peer),
                dst_ref=_place(outs[a], dk, ds, me),
                send_sem=send.at[a, k],
                recv_sem=recv.at[a, k],
                device_id={axis: peer},
                device_id_type=MESH,
            )
            c.start()
            copies.append(c)
    for a, (sk, ss, dk, ds) in enumerate(kinds):
        c = pltpu.make_async_copy(
            _place(ins[a], sk, ss, me), _place(outs[a], dk, ds, me), own.at[a]
        )
        c.start()
        copies.append(c)
    for c in copies:
        c.wait()


def exchange(axis, kinds, ins, out_shapes, cid, source=VMEM):
    n, m = lax.axis_size(axis), len(ins)
    return pl.pallas_call(
        functools.partial(_exchange_kernel, axis, n, kinds),
        out_shape=out_shapes,
        in_specs=[pl.BlockSpec(memory_space=source)] * m,
        out_specs=[pl.BlockSpec(memory_space=VMEM)] * m,
        scratch_shapes=[
            pltpu.SemaphoreType.DMA((m, n - 1)),
            pltpu.SemaphoreType.DMA((m, n - 1)),
            pltpu.SemaphoreType.DMA((m,)),
        ],
        compiler_params=pltpu.CompilerParams(
            collective_id=cid, has_side_effects=True, vmem_limit_bytes=(32 if source is VMEM else 62) << 20
        ),
    )(*ins)


def _around(s):
    c, x, y = lax.rem(s, 2), lax.rem(s // 2, 2), s // 4
    right = s + 2 - 4 * x
    up = s + 4 - 8 * y
    return right, up, up + 2 - 4 * x, 1 - 2 * c


def _gather_kernel(rows, width, in_ref, out_ref, send, recv, own):
    s = lax.axis_index("seq")
    sx, sy, sd, flip = _around(s)
    sib = s + flip
    half = rows // 2

    def at(i, part=None):
        cols = pl.ds(pl.multiple_of(i * width, width), width)
        if part is None:
            return out_ref.at[:, cols]
        return out_ref.at[pl.ds(part * half, half), cols]

    def push(src, dst, to, k):
        c = pltpu.make_async_remote_copy(
            src_ref=src, dst_ref=dst, send_sem=send.at[k], recv_sem=recv.at[k],
            device_id={"seq": to}, device_id_type=MESH,
        )
        c.start()
        return c

    _greet("seq", [sx, sy, sib])
    to_x = push(in_ref, at(s), sx, 0)
    to_y = push(in_ref, at(s), sy, 1)
    to_s = push(in_ref, at(s), sib, 2)
    mine = pltpu.make_async_copy(in_ref, at(s), own)
    mine.start()
    to_x.wait_recv()
    fy = push(at(sx, 0), at(sx, 0), sy, 3)
    gx = push(at(sx), at(sx), sib, 4)
    to_y.wait_recv()
    fx = push(at(sy, 1), at(sy, 1), sx, 5)
    gy = push(at(sy), at(sy), sib, 6)
    fy.wait_recv()
    fx.wait_recv()
    gd = push(at(sd), at(sd), sib, 7)
    to_s.wait_recv()
    gx.wait_recv()
    gy.wait_recv()
    gd.wait_recv()
    for c in (to_x, to_y, to_s, fy, gx, fx, gy, gd):
        c.wait_send()
    mine.wait()


def gather_columns(x, cid):
    rows, width = x.shape
    n = lax.axis_size("seq")
    return pl.pallas_call(
        functools.partial(_gather_kernel, rows, width),
        out_shape=jax.ShapeDtypeStruct((rows, n * width), x.dtype),
        in_specs=[pl.BlockSpec(memory_space=VMEM)],
        out_specs=pl.BlockSpec(memory_space=VMEM),
        scratch_shapes=[
            pltpu.SemaphoreType.DMA((8,)),
            pltpu.SemaphoreType.DMA((8,)),
            pltpu.SemaphoreType.DMA,
        ],
        compiler_params=pltpu.CompilerParams(
            collective_id=cid, has_side_effects=True, vmem_limit_bytes=32 << 20
        ),
    )(x)


def _pusher(send, recv):
    def push(src, dst, to, k):
        c = pltpu.make_async_remote_copy(
            src_ref=src, dst_ref=dst, send_sem=send.at[k], recv_sem=recv.at[k],
            device_id={"seq": to}, device_id_type=MESH,
        )
        c.start()
        return c

    return push


def _up_kernel(
    rows, width, tile, in_ref, gate_hbm, up_hbm, out_ref, all_rows, acc, held, wsem, send, recv, own
):
    s = lax.axis_index("seq")
    sx, sy, sd, flip = _around(s)
    sib = s + flip
    half = rows // 2
    pair = 2 * width
    hidden = out_ref.shape[1]
    chips = [i // 2 for i in (s, sx, sy, sd)]
    _here("seq", [sx, sy, sib])
    loads = []
    for k, chip in enumerate(chips):
        for m, hbm in enumerate((gate_hbm, up_hbm)):
            c = pltpu.make_async_copy(
                hbm.at[0, :, pl.ds(pl.multiple_of(chip * pair, pair), pair)],
                held.at[k, m],
                wsem.at[k, m],
            )
            c.start()
            loads.append(c)
    push = _pusher(send, recv)

    def at(i, part=None):
        cols = pl.ds(pl.multiple_of(i * width, width), width)
        if part is None:
            return all_rows.at[:, cols]
        return all_rows.at[pl.ds(part * half, half), cols]

    def multiply(k):
        loads[2 * k].wait()
        loads[2 * k + 1].wait()
        left = pl.ds(pl.multiple_of(chips[k] * pair, pair), pair)

        @pl.loop(0, hidden // tile)
        def _(j):
            at_j = pl.ds(pl.multiple_of(j * tile, tile), tile)
            x = all_rows[:, left]
            g = times_rows(x, held[k, 0, at_j, :])
            u = times_rows(x, held[k, 1, at_j, :])
            if k:
                g = g + acc[0, :, at_j]
                u = u + acc[1, :, at_j]
            if k < 3:
                acc[0, :, at_j] = g
                acc[1, :, at_j] = u
            else:
                out_ref[:, at_j] = (g / (1.0 + jnp.exp(-g)) * u).astype(out_ref.dtype)

    pl.semaphore_wait(pltpu.get_barrier_semaphore(), 3)
    to_x = push(in_ref, at(s), sx, 0)
    to_y = push(in_ref, at(s), sy, 1)
    to_s = push(in_ref, at(s), sib, 2)
    mine = pltpu.make_async_copy(in_ref, at(s), own)
    mine.start()
    mine.wait()
    to_s.wait_recv()
    multiply(0)
    to_x.wait_recv()
    fy = push(at(sx, 0), at(sx, 0), sy, 3)
    gx = push(at(sx), at(sx), sib, 4)
    to_y.wait_recv()
    fx = push(at(sy, 1), at(sy, 1), sx, 5)
    gy = push(at(sy), at(sy), sib, 6)
    gx.wait_recv()
    multiply(1)
    fy.wait_recv()
    fx.wait_recv()
    gd = push(at(sd), at(sd), sib, 7)
    gy.wait_recv()
    multiply(2)
    gd.wait_recv()
    multiply(3)
    for c in (to_x, to_y, to_s, fy, gx, fx, gy, gd):
        c.wait_send()


def gathered_up(x, w_gate, w_up, cid):
    rows, width = x.shape
    hidden = w_gate.shape[1]
    n = lax.axis_size("seq")
    return pl.pallas_call(
        functools.partial(_up_kernel, rows, width, 384),
        out_shape=jax.ShapeDtypeStruct((rows, hidden), x.dtype),
        in_specs=[pl.BlockSpec(memory_space=VMEM)] + [pl.BlockSpec(memory_space=pl.ANY)] * 2,
        out_specs=pl.BlockSpec(memory_space=VMEM),
        scratch_shapes=[
            VMEM((rows, n * width), x.dtype),
            VMEM((2, rows, hidden), jnp.float32),
            VMEM((4, 2, hidden, 2 * width), x.dtype),
            pltpu.SemaphoreType.DMA((4, 2)),
            pltpu.SemaphoreType.DMA((8,)),
            pltpu.SemaphoreType.DMA((8,)),
            pltpu.SemaphoreType.DMA,
        ],
        compiler_params=pltpu.CompilerParams(
            collective_id=cid, has_side_effects=True, vmem_limit_bytes=52 << 20
        ),
    )(x, w_gate, w_up)


def _down_kernel(
    rows, width, tile, in_ref, down_hbm, out_ref, held, sb, rs, st, so, rd, rx, ry, wsem, send, recv
):
    s = lax.axis_index("seq")
    sx, sy, sd, flip = _around(s)
    sib = s + flip
    half = rows // 2
    step = 32
    order = [sd + flip, sx + flip, sd, sy + flip, sx, sy, s + flip, s]
    _here("seq", [sx, sy, sib])
    loads = []
    for k, i in enumerate(order):
        c = pltpu.make_async_copy(
            down_hbm.at[0, :, pl.ds(pl.multiple_of(i * width, width), width)],
            held.at[k],
            wsem.at[k],
        )
        c.start()
        loads.append(c)
    push = _pusher(send, recv)

    def product(k, dst, more=None):
        loads[k].wait()

        @pl.loop(0, width // tile)
        def _(j):
            at_j = pl.ds(pl.multiple_of(j * tile, tile), tile)
            r = jnp.dot(in_ref[...], held[k, :, at_j], preferred_element_type=jnp.float32)
            if more is not None:
                r = r + more[:, at_j].astype(jnp.float32)
            dst[:, at_j] = r.astype(dst.dtype)

    def add(dst, d0, count, terms):
        @pl.loop(0, count // step)
        def _(i):
            total = None
            for ref, base in terms:
                v = ref[pl.ds(pl.multiple_of(base + i * step, step), step), :].astype(jnp.float32)
                total = v if total is None else total + v
            dst[pl.ds(pl.multiple_of(d0 + i * step, step), step), :] = total.astype(dst.dtype)

    def top(ref):
        return ref.at[pl.ds(0, half), :]

    def bottom(ref):
        return ref.at[pl.ds(half, half), :]

    product(0, sb.at[0])
    pl.semaphore_wait(pltpu.get_barrier_semaphore(), 3)
    cs = [push(sb.at[0], rs.at[0], sib, 0)]
    product(1, sb.at[1])
    cs.append(push(sb.at[1], rs.at[1], sib, 1))
    cs[0].wait_recv()
    product(2, st.at[0], rs.at[0])
    dt = push(top(st.at[0]), rd.at[0], sx, 4)
    db = push(bottom(st.at[0]), rd.at[1], sy, 5)
    product(3, sb.at[2])
    cs.append(push(sb.at[2], rs.at[2], sib, 2))
    cs[1].wait_recv()
    product(4, st.at[1], rs.at[1])
    xt = push(top(st.at[1]), top(rx), sx, 6)
    cs[2].wait_recv()
    product(5, st.at[2], rs.at[2])
    yb = push(bottom(st.at[2]), bottom(ry), sy, 7)
    product(6, sb.at[3])
    cs.append(push(sb.at[3], rs.at[3], sib, 3))
    dt.wait_recv()
    add(st.at[2], 0, half, [(st.at[2], 0), (rd.at[0], 0)])
    yt = push(top(st.at[2]), top(ry), sy, 8)
    db.wait_recv()
    add(st.at[1], half, half, [(st.at[1], half), (rd.at[1], 0)])
    xb = push(bottom(st.at[1]), bottom(rx), sx, 9)
    cs[3].wait_recv()
    product(7, so, rs.at[3])
    xt.wait_recv()
    yt.wait_recv()
    add(out_ref, 0, half, [(so, 0), (rx, 0), (ry, 0)])
    yb.wait_recv()
    xb.wait_recv()
    add(out_ref, half, half, [(so, half), (rx, half), (ry, half)])
    for c in (*cs, dt, db, xt, yb, yt, xb):
        c.wait_send()


def down_scattered(x, w_down, cid):
    rows, hidden = x.shape
    n = lax.axis_size("seq")
    width = w_down.shape[2] // n
    b = x.dtype
    return pl.pallas_call(
        functools.partial(_down_kernel, rows, width, 256),
        out_shape=jax.ShapeDtypeStruct((rows, width), b),
        in_specs=[pl.BlockSpec(memory_space=VMEM), pl.BlockSpec(memory_space=pl.ANY)],
        out_specs=pl.BlockSpec(memory_space=VMEM),
        scratch_shapes=[
            VMEM((n, hidden, width), b),
            VMEM((4, rows, width), b),
            VMEM((4, rows, width), b),
            VMEM((3, rows, width), b),
            VMEM((rows, width), jnp.float32),
            VMEM((2, rows // 2, width), b),
            VMEM((rows, width), b),
            VMEM((rows, width), b),
            pltpu.SemaphoreType.DMA((n,)),
            pltpu.SemaphoreType.DMA((10,)),
            pltpu.SemaphoreType.DMA((10,)),
        ],
        compiler_params=pltpu.CompilerParams(
            collective_id=cid, has_side_effects=True, vmem_limit_bytes=52 << 20
        ),
    )(x, w_down)


def by_heads(
    query_proj,
    key_proj,
    value_proj,
    residual,
    out_weight,
    expert_ids,
    gate_values,
    w_gate,
    w_up,
    w_down,
):
    n_seq, groups = lax.axis_size("seq"), lax.axis_size("exp")
    block = query_proj.shape[0]
    tokens = n_seq * block
    tok_sub = residual.shape[0]
    width = residual.shape[1] // n_seq
    plane = n_seq * tok_sub
    capacity = max(2, (3 * tok_sub * TOP + 2 * groups - 1) // (2 * groups))
    bf, f32 = jnp.bfloat16, jnp.float32
    meta = jnp.concatenate(
        [expert_ids.T.astype(f32), gate_values.T, jnp.zeros((8 - 2 * TOP, tok_sub), f32)], axis=0
    )
    meta = jnp.pad(meta, ((0, 0), (0, 128 - tok_sub)))
    head = ("col", HD, "row", block)
    q, k, v, res, meta = exchange(
        "seq",
        (head, head, head, ("col", width, "row", tok_sub), ("all", 0, "row", 8)),
        (query_proj, key_proj, value_proj, residual, meta),
        [jax.ShapeDtypeStruct((tokens, HD), bf)] * 3
        + [jax.ShapeDtypeStruct((plane, width), bf), jax.ShapeDtypeStruct((8 * n_seq, 128), f32)],
        0,
        pl.ANY,
    )
    qf = features(q).reshape(n_seq, block, HD)
    kf = features(k).reshape(n_seq, block, HD)
    vr = v.reshape(n_seq, block, HD)
    states = jnp.einsum("btd,bte->bde", kf, vr, preferred_element_type=f32)
    running, before_it = jnp.zeros_like(states[0]), []
    for b in range(n_seq):
        before_it.append(running)
        running = running + states[b]
    prefix = jnp.stack(before_it).astype(bf)
    scores = jnp.einsum("btd,bsd->bts", qf, kf, preferred_element_type=f32)
    causal = jnp.arange(block)[:, None] >= jnp.arange(block)[None, :]
    weights = jnp.where(causal[None], scores, 0.0).astype(bf)
    combined = jnp.einsum("bts,bse->bte", weights, vr, preferred_element_type=f32)
    combined = combined + jnp.einsum("btd,bde->bte", qf, prefix, preferred_element_type=f32)
    normed = combined * lax.rsqrt(jnp.mean(combined * combined, axis=-1, keepdims=True) + 1e-06)
    normed = normed.astype(bf).reshape(n_seq, groups, tok_sub, HD)
    normed = normed.transpose(1, 0, 2, 3).reshape(tokens, HD)

    partial_out = times_rows(gather_columns(normed, 1), out_weight).astype(bf)
    (parts,) = exchange(
        "exp",
        (("row", plane, "row", plane),),
        (partial_out,),
        [jax.ShapeDtypeStruct((tokens, width), bf)],
        2,
    )
    summed = jnp.sum(parts.reshape(groups, plane, width).astype(f32), axis=0)
    mixed_in = (res.astype(f32) + summed).astype(bf)

    meta = meta.reshape(n_seq, 8, 128)
    ids = meta[:, :TOP, :tok_sub].astype(jnp.int32).transpose(0, 2, 1)
    gates = meta[:, TOP : 2 * TOP, :tok_sub].transpose(0, 2, 1).reshape(plane, TOP)
    chosen = ids.reshape(n_seq, tok_sub * TOP)
    onehot = (chosen[:, :, None] == jnp.arange(groups, dtype=jnp.int32)).astype(jnp.int32)
    earlier = (jnp.arange(tok_sub * TOP)[:, None] > jnp.arange(tok_sub * TOP)[None, :])
    before = jnp.sum(earlier[None, :, :, None] * onehot[:, None, :, :], axis=2)
    slot = jnp.sum(before * onehot, axis=2)
    target = (chosen * n_seq + jnp.arange(n_seq, dtype=jnp.int32)[:, None]) * capacity + slot
    target = target.reshape(plane, TOP)
    slots = jnp.arange(groups * n_seq * capacity, dtype=jnp.int32)
    picks = [(target[:, j : j + 1] == slots[None, :]).astype(bf) for j in range(TOP)]
    placing = picks[0]
    for p in picks[1:]:
        placing = placing + p
    outgoing = lax.dot_general(
        placing, mixed_in, (((0,), (0,)), ((), ())), preferred_element_type=f32
    ).astype(bf)
    load = n_seq * capacity
    rows_shape = [jax.ShapeDtypeStruct((groups * load, width), bf)]
    (arrived,) = exchange("exp", (("row", load, "row", load),), (outgoing,), rows_shape, 3)
    activated = gathered_up(arrived, w_gate, w_up, 4)
    sums = down_scattered(activated, w_down, 5)
    (returned,) = exchange("exp", (("row", load, "row", load),), (sums,), rows_shape, 6)
    mixed = mixed_in.astype(f32)
    extra = jnp.zeros_like(mixed)
    for j in range(TOP):
        picked = jnp.dot(picks[j], returned, preferred_element_type=f32)
        extra = extra + gates[:, j : j + 1] * picked
    mixed = (mixed + extra).astype(bf)
    (out,) = exchange(
        "seq",
        (("row", tok_sub, "col", width),),
        (mixed,),
        [jax.ShapeDtypeStruct(residual.shape, bf)],
        7,
    )
    return out


def solution(mesh):
    return jax.shard_map(
        by_heads if mesh.shape["seq"] == 8 and mesh.shape["exp"] == 4 else local,
        mesh=mesh,
        in_specs=(
            P("seq", "exp"),
            P("seq", "exp"),
            P("seq", "exp"),
            P(("seq", "exp"), None),
            P("seq", "exp"),
            P(("seq", "exp"), None),
            P(("seq", "exp"), None),
            P("exp", "seq", None),
            P("exp", "seq", None),
            P("exp", "seq", None),
        ),
        out_specs=P(("seq", "exp"), None),
        check_vma=False,
    )
```
